32 devices in a mesh: field: 2 (over x), tile: 16 (over z, y, core).
Axes of the slice: x: 2, y: 2, z: 4, core: 2. Of those that a mesh axis runs over, the one named last changes fastest.
Arguments:
- psi_det: float32 [128, 8, 8, 128], P(('field', 'tile')), parts along dimension 0, may hold values from -6 to 6
- phi_det: float32 [128, 8, 8, 128], P(('field', 'tile')), parts along dimension 0, may hold values from 0.25 to 4
- dest_tile: int32 [128, 8, 1], P(('field', 'tile')), parts along dimension 0, may hold values from 0 to 15; in each aligned block of 32 rows (0 to 31, 32 to 63, ..., all dimensions but the last counted through in order) at most 4 rows name the same one
- dest_cell: int32 [128, 8], P(('field', 'tile')), parts along dimension 0, may hold values from 0 to 3
- kernel_id: int32 [128, 8], P(('field', 'tile')), parts along dimension 0, may hold values from 0 to 7
- intersection_weight: float32 [128, 8], P(('field', 'tile')), parts along dimension 0, may hold values from 0.5 to 1.5
- kernels: float32 [8, 128, 128], replicated, may hold values from 0 to 2
- row_offsets: int32 [16, 16], P('field'), parts along dimension 0, may hold values from -8 to 8
- col_offsets: int32 [16, 16], P('field'), parts along dimension 0, may hold values from -64 to 64
Outputs:
- best: float32 [256, 512], P(('field', 'tile')), parts along dimension 0
The draws below stay inside these ranges and needn't reach their ends.
There are 2 independent parts, one for each index of `field`. The reference program is written for one: setup_inputs(seed, part) draws one part's arguments, and reference() takes and returns one part's arrays. A program takes and returns all parts, laid end to end along the dimension named above; an argument that names none is the same for every part. Nothing has to cross between parts.
Inputs may be any that keep to these rules, and one draw needn't show every extreme that they name: `dest_tile`: among one device's 4 blocks over all 8 epochs no tile is named more than 4 times, a bound that some block reaches. `kernels`: every kernel is tridiagonal; kernels[k, i, j] = 0 whenever |i - j| > 1.
All inputs are finite; a program needn't handle non-finite values.
Results may differ from the reference program's by a relative error of at most 0.0003.
Values sent between devices are 32-bit elements; how exact they have to be, the bound alone decides.
No kernel may reach another device: no remote copies, remote signals or barrier semaphores. Data moves between devices by JAX's collectives and lax.ppermute only.
A program may use at most 64 MiB of HBM per device.

```python
import math
import jax
import jax.numpy as jnp
import numpy as np
from jax import lax

ROWS = 8
CELLS = 4
BLOCKW = 128
EPOCHS = 8
VELS = 16
KERNELS = 8
XREACH = 64
RREACH = 8
CAP = 4
BLOCKS = 64
N_TILE = 16


def draw_kernels(key, part):
    key_main = jax.random.fold_in(key, 101)
    key_upper = jax.random.fold_in(key, 202)
    key_lower = jax.random.fold_in(key, 303)
    main = jax.random.uniform(key_main, (KERNELS, BLOCKW), jnp.float32, 1.0, 2.0)
    upper = jax.random.uniform(key_upper, (KERNELS, BLOCKW), jnp.float32, 0.1, 0.5)
    lower = jax.random.uniform(key_lower, (KERNELS, BLOCKW), jnp.float32, 0.1, 0.5)
    positions = jnp.arange(BLOCKW)
    diagonal_mask = (positions[:, None] == positions[None, :]).astype(jnp.float32)
    upper_mask = (positions[None, :] == positions[:, None] + 1).astype(jnp.float32)
    lower_mask = (positions[None, :] == positions[:, None] - 1).astype(jnp.float32)
    return main[:, :, None] * diagonal_mask + upper[:, :, None] * upper_mask + lower[:, :, None] * lower_mask


def set_ends(values, stream_key, least, high):
    place = [jax.random.randint(jax.random.fold_in(stream_key, axis), (), 0, length) for axis, length in enumerate(values.shape)]
    main_axis = values.shape.index(max(values.shape))
    beside = place[:main_axis] + [(place[main_axis] + 1) % values.shape[main_axis]] + place[main_axis + 1:]
    return values.at[tuple(place)].set(least).at[tuple(beside)].set(high)


def level_of(key, extent, cuts, least, high):
    def one(position, blocks):
        draws = jax.random.uniform(jax.random.fold_in(jax.random.fold_in(key, 6), position), (blocks,), jnp.float32, least / len(cuts), high / len(cuts))
        return jnp.repeat(jnp.exp(draws), extent[position] // blocks).reshape((-1,) + (1,) * (len(extent) - position - 1))

    factor_of = one(*cuts[0])
    for cut in cuts[1:]:
        factor_of = factor_of * one(*cut)
    return factor_of


def deal_out(rng, own, number, rows, number_of, top, most, skew):
    ranking = jax.random.permutation(rng, number_of)
    packed, ordinary = shares(number_of, rows * top, most, skew, True), shares(number_of, rows * top, most, skew, False)
    places = jnp.arange(number_of)

    def named(tallies, turn):
        used = int((tallies > 0).sum())
        fixed = max(1, used // 4)
        passed = fixed + (places - fixed + turn * (used - fixed)) % max(1, number_of - fixed)
        return jnp.zeros((number_of,), jnp.int32).at[ranking[jnp.where(places < fixed, places, passed)]].set(jnp.asarray(tallies, jnp.int32))

    tallies = jnp.where(number % 4 == 0, named(packed, number // 4), named(ordinary, number - number // 4 - 1))
    mixed = jax.random.permutation(jax.random.fold_in(own, 3), number_of)
    donor, receiver = mixed[0:number_of // 2 * 2:2], mixed[1:number_of // 2 * 2:2]
    room = jnp.minimum(tallies[donor] - 1, most - tallies[receiver]) // 2
    room = jnp.where((donor == ranking[0]) | (receiver == ranking[0]) | (tallies[receiver] == 0), 0, jnp.maximum(room, 0))
    passed = jax.random.randint(jax.random.fold_in(own, 4), (number_of // 2,), 0, 1 << 20) % (room + 1)
    tallies = tallies.at[donor].add(-passed).at[receiver].add(passed)
    labels = jnp.searchsorted(jnp.cumsum(tallies), jnp.arange(rows * top), side="right").astype(jnp.int32)
    table = labels.reshape(top, rows).T
    table = table[jax.random.permutation(jax.random.fold_in(own, 1), rows)]
    turn = jax.random.randint(jax.random.fold_in(own, 2), (rows, 1), 0, top)
    return jnp.take_along_axis(table, (jnp.arange(top)[None, :] + turn) % top, axis=1)


def shares(count, total, limit, skew, full):
    loads = [(1 << 20) // math.isqrt(rank ** skew) + 1 for rank in range(1, count + 1)]
    largest = limit if full else min(limit, max(-(-total // count), total * loads[0] // sum(loads)))
    least = 1 if total - largest >= count - 1 else 0
    counts, rest = [largest] + [least] * (count - 1), total - largest - least * (count - 1)
    while rest > 0:
        free = [i for i in range(1, count) if counts[i] < largest] or [i for i in range(1, count) if counts[i] < limit]
        pool, left = sum([loads[i] for i in free]), rest
        for i in free:
            more = min(limit - counts[i], max(1, left * loads[i] // pool), rest)
            counts[i] = counts[i] + more
            rest = rest - more
    return np.array(counts)


def bell_draw(rng, extent, spread, most, cuts=(), kind=jnp.bfloat16):
    array = spread * jax.random.normal(rng, extent, jnp.float32)
    if cuts:
        array = array * level_of(rng, extent, cuts, -0.22, 0.18)
    return jnp.clip(array, -most, most).astype(kind)


def setup_inputs(seed: int = 0, part: int = 0) -> dict:
    splits = jax.random.split(jax.random.key(seed), 10)
    own_keys = jax.random.split(jax.random.fold_in(splits[9], part), 10)
    psi_det = bell_draw(own_keys[0], (BLOCKS, EPOCHS, ROWS, BLOCKW), 1.0, 6.0, ((0, 16),), jnp.float32)
    phi_det = jnp.clip(jnp.exp(math.log(4.0) - 2.7725887 * jax.random.uniform(own_keys[1], (BLOCKS, EPOCHS, ROWS, BLOCKW), jnp.float32) ** level_of(own_keys[1], (BLOCKS, EPOCHS, ROWS, BLOCKW), ((0, 16),), -0.2, 0.2)), 0.25, 4.0)
    dest_tile_keys = jax.random.split(jax.random.fold_in(own_keys[2], 1), BLOCKS * EPOCHS // (CELLS * EPOCHS))
    dest_tile_turns = jax.random.permutation(jax.random.fold_in(own_keys[2], 3), BLOCKS * EPOCHS // (CELLS * EPOCHS))
    dest_tile = jax.vmap(lambda own, number: deal_out(jax.random.fold_in(own_keys[2], 2), own, number, CELLS * EPOCHS, N_TILE, 1, CAP, 2))(dest_tile_keys, dest_tile_turns).reshape((BLOCKS, EPOCHS, 1))
    dest_cell = set_ends(jax.random.randint(own_keys[3], (BLOCKS, EPOCHS), 0, CELLS), jax.random.fold_in(own_keys[3], 1), 0, CELLS - 1).astype(jnp.int32)
    kernel_id = set_ends(jax.random.randint(own_keys[4], (BLOCKS, EPOCHS), 0, KERNELS), jax.random.fold_in(own_keys[4], 1), 0, KERNELS - 1).astype(jnp.int32)
    intersection_weight = jnp.clip(0.5 + 1.0 * jax.random.uniform(own_keys[5], (BLOCKS, EPOCHS), jnp.float32) ** level_of(own_keys[5], (BLOCKS, EPOCHS), ((0, 16),), -0.2, 0.2), 0.5, 1.5)
    kernels = draw_kernels(jax.random.fold_in(splits[9], 71), part)
    row_offsets = set_ends(jax.random.randint(own_keys[7], (EPOCHS, VELS), 0 - RREACH, RREACH + 1), jax.random.fold_in(own_keys[7], 1), 0 - RREACH, RREACH).astype(jnp.int32)
    col_offsets = set_ends(jax.random.randint(own_keys[8], (EPOCHS, VELS), 0 - XREACH, XREACH + 1), jax.random.fold_in(own_keys[8], 1), 0 - XREACH, XREACH).astype(jnp.int32)
    return {"psi_det": psi_det, "phi_det": phi_det, "dest_tile": dest_tile, "dest_cell": dest_cell, "kernel_id": kernel_id, "intersection_weight": intersection_weight, "kernels": kernels, "row_offsets": row_offsets, "col_offsets": col_offsets}


def reproject(payload, kernel_ids, weights, kernels_table):
    row_total = payload.shape[0]
    group_size = math.gcd(row_total, 32)

    def one_group(group_items):
        pieces, chosen_ids, factors = group_items
        chosen = kernels_table[chosen_ids]
        moved = jnp.einsum('ncrb,nbk->ncrk', pieces, chosen, precision=lax.Precision.HIGHEST)
        return moved * factors[:, None, None, None]
    grouped = (payload.reshape((row_total // group_size, group_size) + payload.shape[1:]), kernel_ids.reshape(row_total // group_size, group_size), weights.reshape(row_total // group_size, group_size))
    return lax.map(one_group, grouped).reshape(payload.shape)

def reference(psi_det, phi_det, dest_tile, dest_cell, kernel_id, intersection_weight, kernels, row_offsets, col_offsets):
    block_count = psi_det.shape[0]
    row_total = block_count * EPOCHS
    blocks = jnp.stack([psi_det, phi_det], axis=2).reshape(row_total, 2, ROWS, BLOCKW)
    moved = reproject(blocks, kernel_id.reshape(row_total).astype(jnp.int32), intersection_weight.reshape(row_total), kernels)
    epoch_of = jnp.arange(row_total, dtype=jnp.int32) % EPOCHS
    target = (dest_tile.reshape(row_total).astype(jnp.int32) * EPOCHS + epoch_of) * CELLS + dest_cell.reshape(row_total).astype(jnp.int32)
    summed = jax.ops.segment_sum(moved.reshape(row_total, -1), target, num_segments=N_TILE * EPOCHS * CELLS)
    sky_image = summed.reshape(N_TILE, EPOCHS, CELLS, 2, ROWS, BLOCKW).transpose(3, 1, 0, 4, 2, 5)
    total_rows = N_TILE * ROWS
    side_cols = CELLS * BLOCKW
    sky_image = sky_image.reshape(2, EPOCHS, total_rows, side_cols)
    padded = jnp.pad(sky_image, ((0, 0), (0, 0), (RREACH, RREACH), (XREACH, XREACH)))

    def one_velocity(highest, offsets):
        row_shift, col_shift = offsets
        sums = jnp.zeros((2, total_rows, side_cols), jnp.float32)
        for epoch_idx in range(EPOCHS):
            start_row = (RREACH + row_shift[epoch_idx]).astype(jnp.int32)
            start_col = (XREACH + col_shift[epoch_idx]).astype(jnp.int32)
            sums = sums + lax.dynamic_slice(padded[:, epoch_idx], (jnp.int32(0), start_row, start_col), (2, total_rows, side_cols))
        score = sums[0] / jnp.sqrt(jnp.maximum(sums[1], 1.0))
        return (jnp.maximum(highest, score), None)
    start = jnp.full((total_rows, side_cols), -jnp.inf, jnp.float32)
    result = lax.scan(one_velocity, start, (row_offsets.T, col_offsets.T))
    return result[0]
```

```python
import functools

import jax
import jax.numpy as jnp
from jax import lax
from jax.experimental import pallas as pl
from jax.experimental.pallas import tpu as pltpu
from jax.sharding import PartitionSpec as P

XREACH = 64
RREACH = 8
LANES = 128
VMEM = pl.BlockSpec(memory_space=pltpu.VMEM)
SMEM = pl.BlockSpec(memory_space=pltpu.SMEM)
LIMIT = pltpu.CompilerParams(vmem_limit_bytes=32 * 1024 * 1024)


def pack_kernel(
    capacity, tile_ref, cell_ref, id_ref, weight_ref, psi_ref, phi_ref, table_ref, out_ref, diag_ref, used_ref
):
    cells, epochs = psi_ref.shape[:2]
    tiles, width = out_ref.shape[0], psi_ref.shape[3]

    source = lax.broadcasted_iota(jnp.int32, (width, width), 0)
    target = lax.broadcasted_iota(jnp.int32, (width, width), 1)
    for place in range(3):
        mask = source == target + (place - 1)
        for index in range(table_ref.shape[0]):
            row = jnp.sum(jnp.where(mask, table_ref[index], 0.0), axis=0, keepdims=True)
            diag_ref[index, place : place + 1, :] = row

    def clear(tile, carry):
        used_ref[tile] = 0
        out_ref[tile, 2 * capacity] = jnp.zeros(out_ref.shape[2:], jnp.float32)
        return carry

    lax.fori_loop(0, tiles, clear, 0)
    lane = lax.broadcasted_iota(jnp.int32, (1, LANES), 1)
    for block in range(cells):
        for epoch in range(epochs):
            tile = tile_ref[block, epoch, 0]
            slot = used_ref[tile]
            used_ref[tile] = slot + 1
            bands = diag_ref[id_ref[block, epoch]] * weight_ref[block, epoch]
            for kind, ref in enumerate((psi_ref, phi_ref)):
                values = ref[block, epoch]
                out_ref[tile, 2 * slot + kind] = (
                    values * bands[1:2]
                    + pltpu.roll(values, 1, 1) * bands[0:1]
                    + pltpu.roll(values, width - 1, 1) * bands[2:3]
                )
            place = (epoch * 2 * cells + cell_ref[block, epoch] + 1).astype(jnp.float32)
            note = out_ref[tile, 2 * capacity, 0:1, :]
            out_ref[tile, 2 * capacity, 0:1, :] = jnp.where(lane == slot, place, note)


def sum_kernel(capacity, cells, in_ref, sky_ref):
    for index in range(sky_ref.shape[0]):
        sky_ref[index] = jnp.zeros(sky_ref.shape[1:], jnp.float32)

    def one_source(source, carry):
        notes = in_ref[source, 2 * capacity].astype(jnp.int32)
        for slot in range(capacity):
            place = notes[0, slot] - 1
            there = place >= 0
            base = jnp.maximum(place, 0)
            for kind in range(2):
                value = jnp.where(there, in_ref[source, 2 * slot + kind], 0.0)
                sky_ref[base + kind * cells] = sky_ref[base + kind * cells] + value
        return carry

    lax.fori_loop(0, in_ref.shape[0], one_source, 0, unroll=4)


def stack_kernel(cells, row_ref, col_ref, odd_ref, own_ref, twin_ref, far_ref, best_ref, wide_ref):
    epochs, vels = row_ref.shape
    rows = own_ref.shape[1]
    odd = odd_ref[0]
    twin_row = pl.multiple_of((1 - odd) * 2 * rows, rows)
    far_row = pl.multiple_of(odd * 2 * rows, rows)
    for epoch in range(epochs):
        for kind in range(2):
            zeros = jnp.zeros(wide_ref.shape[3:], jnp.float32)
            wide_ref[epoch, kind, 0] = zeros
            wide_ref[epoch, kind, cells + 1] = zeros
            for cell in range(cells):
                index = (epoch * 2 + kind) * cells + cell
                wide_ref[epoch, kind, cell + 1, rows : 2 * rows, :] = own_ref[index]
                wide_ref[epoch, kind, cell + 1, pl.ds(twin_row, rows), :] = twin_ref[index]
                wide_ref[epoch, kind, cell + 1, pl.ds(far_row, rows), :] = far_ref[index]
    lane = lax.broadcasted_iota(jnp.int32, (rows, LANES), 1)

    def one_velocity(vel, highest):
        sums = [[jnp.zeros((rows, LANES), jnp.float32) for _ in range(cells)] for _ in range(2)]
        for epoch in range(epochs):
            start_row = rows + row_ref[epoch, vel]
            start_col = LANES + col_ref[epoch, vel]
            first = lax.shift_right_logical(start_col, 7)
            shift = start_col & (LANES - 1)
            mask = lane >= shift
            turn = (LANES - shift) & (LANES - 1)
            for kind in range(2):
                parts = [
                    wide_ref[epoch, kind, first + step, pl.ds(start_row, rows), :]
                    for step in range(cells + 1)
                ]
                for cell in range(cells):
                    merged = jnp.where(mask, parts[cell], parts[cell + 1])
                    sums[kind][cell] = sums[kind][cell] + pltpu.roll(merged, turn, 1)
        return [
            jnp.maximum(highest[cell], sums[0][cell] / jnp.sqrt(jnp.maximum(sums[1][cell], 1.0)))
            for cell in range(cells)
        ]

    start = [jnp.full((rows, LANES), -jnp.inf, jnp.float32) for _ in range(cells)]
    highest = lax.fori_loop(0, vels, one_velocity, start)
    for cell in range(cells):
        best_ref[:, cell * LANES : (cell + 1) * LANES] = highest[cell]


def body(psi, phi, dest_tile, dest_cell, kernel_id, weight, kernels, row_offsets, col_offsets):
    tiles = lax.axis_size("tile")
    cells, epochs, rows, width = psi.shape
    capacity = max(2, 2 * cells * epochs // tiles)
    message = (tiles, 2 * capacity + 1, rows, width)
    outgoing = pl.pallas_call(
        functools.partial(pack_kernel, capacity),
        out_shape=jax.ShapeDtypeStruct(message, jnp.float32),
        in_specs=[SMEM] * 4 + [VMEM] * 3,
        out_specs=VMEM,
        scratch_shapes=[
            pltpu.VMEM((kernels.shape[0], 3, width), jnp.float32),
            pltpu.SMEM((tiles,), jnp.int32),
        ],
        compiler_params=LIMIT,
        name="pack",
    )(dest_tile, dest_cell, kernel_id, weight, psi, phi, kernels)
    incoming = lax.all_to_all(outgoing, "tile", split_axis=0, concat_axis=0, tiled=True)
    sky = pl.pallas_call(
        functools.partial(sum_kernel, capacity, cells),
        out_shape=jax.ShapeDtypeStruct((epochs * 2 * cells, rows, width), jnp.float32),
        in_specs=[VMEM],
        out_specs=VMEM,
        compiler_params=LIMIT,
        name="sum_slots",
    )(incoming)
    twin = lax.ppermute(sky, "tile", [(i, i ^ 1) for i in range(tiles)])
    far = lax.ppermute(
        sky, "tile", [pair for i in range(1, tiles - 1, 2) for pair in ((i, i + 1), (i + 1, i))]
    )
    odd = (lax.axis_index("tile") & 1).reshape(1)
    return pl.pallas_call(
        functools.partial(stack_kernel, cells),
        out_shape=jax.ShapeDtypeStruct((rows, cells * width), jnp.float32),
        in_specs=[SMEM] * 3 + [VMEM] * 3,
        out_specs=VMEM,
        scratch_shapes=[pltpu.VMEM((epochs, 2, cells + 2, 3 * rows, width), jnp.float32)],
        compiler_params=LIMIT,
        name="stack",
    )(row_offsets, col_offsets, odd, sky, twin, far)


def solution(mesh):
    placed = (
        P(("field", "tile"), None, None, None),
        P(("field", "tile"), None, None, None),
        P(("field", "tile"), None, None),
        P(("field", "tile"), None),
        P(("field", "tile"), None),
        P(("field", "tile"), None),
        P(),
        P("field", None),
        P("field", None),
    )
    return jax.shard_map(
        body, mesh=mesh, in_specs=placed, out_specs=P(("field", "tile"), None), check_vma=False
    )
```

```python
import functools

import jax
import jax.numpy as jnp
from jax import lax
from jax.experimental import pallas as pl
from jax.experimental.pallas import tpu as pltpu
from jax.sharding import PartitionSpec as P

XREACH = 64
RREACH = 8
LANES = 128
VMEM = pl.BlockSpec(memory_space=pltpu.VMEM)
SMEM = pl.BlockSpec(memory_space=pltpu.SMEM)
LIMIT = pltpu.CompilerParams(vmem_limit_bytes=32 * 1024 * 1024)


def pack_kernel(capacity, *refs):
    given, out_ref, (diag_ref, used_ref), held, sems = refs[:7], refs[7], refs[8:10], refs[10:17], refs[17]
    copies = [
        pltpu.make_async_copy(source, target, sems.at[index])
        for index, (source, target) in enumerate(zip(given, held, strict=True))
    ]
    for copy in copies:
        copy.start()
    tile_ref, cell_ref, id_ref, weight_ref, psi_ref, phi_ref, table_ref = held
    cells, epochs = psi_ref.shape[:2]
    tiles, width = out_ref.shape[0], psi_ref.shape[3]

    def clear(tile, carry):
        used_ref[tile] = 0
        out_ref[tile, 2 * capacity] = jnp.zeros(out_ref.shape[2:], jnp.float32)
        return carry

    lax.fori_loop(0, tiles, clear, 0)
    for copy in copies:
        copy.wait()

    source = lax.broadcasted_iota(jnp.int32, (width, width), 0)
    target = lax.broadcasted_iota(jnp.int32, (width, width), 1)
    for place in range(3):
        mask = source == target + (place - 1)
        for index in range(table_ref.shape[0]):
            row = jnp.sum(jnp.where(mask, table_ref[index], 0.0), axis=0, keepdims=True)
            diag_ref[index, place : place + 1, :] = row

    lane = lax.broadcasted_iota(jnp.int32, (1, LANES), 1)
    for block in range(cells):
        for epoch in range(epochs):
            tile = tile_ref[block, 0, epoch]
            slot = used_ref[tile]
            used_ref[tile] = slot + 1
            bands = diag_ref[id_ref[block, epoch]] * weight_ref[block, epoch]
            for kind, ref in enumerate((psi_ref, phi_ref)):
                values = ref[block, epoch]
                out_ref[tile, 2 * slot + kind] = (
                    values * bands[1:2]
                    + pltpu.roll(values, 1, 1) * bands[0:1]
                    + pltpu.roll(values, width - 1, 1) * bands[2:3]
                )
            place = (epoch * 2 * cells + cell_ref[block, epoch] + 1).astype(jnp.float32)
            note = out_ref[tile, 2 * capacity, 0:1, :]
            out_ref[tile, 2 * capacity, 0:1, :] = jnp.where(lane == slot, place, note)


def sum_kernel(capacity, cells, in_ref, sky_ref):
    for index in range(sky_ref.shape[0]):
        sky_ref[index] = jnp.zeros(sky_ref.shape[1:], jnp.float32)

    def one_source(source, carry):
        notes = in_ref[source, 2 * capacity].astype(jnp.int32)
        for slot in range(capacity):
            place = notes[0, slot] - 1
            there = place >= 0
            base = jnp.maximum(place, 0)
            for kind in range(2):
                value = jnp.where(there, in_ref[source, 2 * slot + kind], 0.0)
                sky_ref[base + kind * cells] = sky_ref[base + kind * cells] + value
        return carry

    lax.fori_loop(0, in_ref.shape[0], one_source, 0, unroll=4)


def stack_kernel(cells, row_ref, col_ref, odd_ref, own_ref, twin_ref, far_ref, best_ref, wide_ref):
    epochs, vels = row_ref.shape
    rows = own_ref.shape[1]
    odd = odd_ref[0]
    twin_row = pl.multiple_of((1 - odd) * 2 * rows, rows)
    far_row = pl.multiple_of(odd * 2 * rows, rows)
    for epoch in range(epochs):
        for kind in range(2):
            zeros = jnp.zeros(wide_ref.shape[3:], jnp.float32)
            wide_ref[epoch, kind, 0] = zeros
            wide_ref[epoch, kind, cells + 1] = zeros
            for cell in range(cells):
                index = (epoch * 2 + kind) * cells + cell
                wide_ref[epoch, kind, cell + 1, rows : 2 * rows, :] = own_ref[index]
                wide_ref[epoch, kind, cell + 1, pl.ds(twin_row, rows), :] = twin_ref[index]
                wide_ref[epoch, kind, cell + 1, pl.ds(far_row, rows), :] = far_ref[index]
    lane = lax.broadcasted_iota(jnp.int32, (rows, LANES), 1)

    def one_velocity(vel, highest):
        sums = [[jnp.zeros((rows, LANES), jnp.float32) for _ in range(cells)] for _ in range(2)]
        for epoch in range(epochs):
            start_row = rows + row_ref[epoch, vel]
            start_col = LANES + col_ref[epoch, vel]
            first = lax.shift_right_logical(start_col, 7)
            shift = start_col & (LANES - 1)
            mask = lane >= shift
            turn = (LANES - shift) & (LANES - 1)
            for kind in range(2):
                parts = [
                    wide_ref[epoch, kind, first + step, pl.ds(start_row, rows), :]
                    for step in range(cells + 1)
                ]
                for cell in range(cells):
                    merged = jnp.where(mask, parts[cell], parts[cell + 1])
                    sums[kind][cell] = sums[kind][cell] + pltpu.roll(merged, turn, 1)
        return [
            jnp.maximum(highest[cell], sums[0][cell] / jnp.sqrt(jnp.maximum(sums[1][cell], 1.0)))
            for cell in range(cells)
        ]

    start = [jnp.full((rows, LANES), -jnp.inf, jnp.float32) for _ in range(cells)]
    highest = lax.fori_loop(0, vels, one_velocity, start, unroll=4)
    for cell in range(cells):
        best_ref[:, cell * LANES : (cell + 1) * LANES] = highest[cell]


def body(psi, phi, dest_tile, dest_cell, kernel_id, weight, kernels, row_offsets, col_offsets):
    tiles = lax.axis_size("tile")
    cells, epochs, rows, width = psi.shape
    capacity = max(2, 2 * cells * epochs // tiles)
    message = (tiles, 2 * capacity + 1, rows, width)
    given = (jnp.swapaxes(dest_tile, 1, 2), dest_cell, kernel_id, weight, psi, phi, kernels)
    outgoing = pl.pallas_call(
        functools.partial(pack_kernel, capacity),
        out_shape=jax.ShapeDtypeStruct(message, jnp.float32),
        in_specs=[pl.BlockSpec(memory_space=pl.ANY)] * 7,
        out_specs=VMEM,
        scratch_shapes=[
            pltpu.VMEM((kernels.shape[0], 3, width), jnp.float32),
            pltpu.SMEM((tiles,), jnp.int32),
        ]
        + [pltpu.SMEM(array.shape, array.dtype) for array in given[:4]]
        + [pltpu.VMEM(array.shape, array.dtype) for array in given[4:]]
        + [pltpu.SemaphoreType.DMA((7,))],
        compiler_params=pltpu.CompilerParams(vmem_limit_bytes=60 * 1024 * 1024),
        name="pack",
    )(*given)
    incoming = lax.all_to_all(outgoing, "tile", split_axis=0, concat_axis=0, tiled=True)
    sky = pl.pallas_call(
        functools.partial(sum_kernel, capacity, cells),
        out_shape=jax.ShapeDtypeStruct((epochs * 2 * cells, rows, width), jnp.float32),
        in_specs=[VMEM],
        out_specs=VMEM,
        compiler_params=LIMIT,
        name="sum_slots",
    )(incoming)
    twin = lax.ppermute(sky, "tile", [(i, i ^ 1) for i in range(tiles)])
    far = lax.ppermute(
        sky, "tile", [pair for i in range(1, tiles - 1, 2) for pair in ((i, i + 1), (i + 1, i))]
    )
    odd = (lax.axis_index("tile") & 1).reshape(1)
    return pl.pallas_call(
        functools.partial(stack_kernel, cells),
        out_shape=jax.ShapeDtypeStruct((rows, cells * width), jnp.float32),
        in_specs=[SMEM] * 3 + [VMEM] * 3,
        out_specs=VMEM,
        scratch_shapes=[pltpu.VMEM((epochs, 2, cells + 2, 3 * rows, width), jnp.float32)],
        compiler_params=LIMIT,
        name="stack",
    )(row_offsets, col_offsets, odd, sky, twin, far)


def solution(mesh):
    placed = (
        P(("field", "tile"), None, None, None),
        P(("field", "tile"), None, None, None),
        P(("field", "tile"), None, None),
        P(("field", "tile"), None),
        P(("field", "tile"), None),
        P(("field", "tile"), None),
        P(),
        P("field", None),
        P("field", None),
    )
    return jax.shard_map(
        body, mesh=mesh, in_specs=placed, out_specs=P(("field", "tile"), None), check_vma=False
    )
```

```python
import functools

import jax
import jax.numpy as jnp
from jax import lax
from jax.experimental import pallas as pl
from jax.experimental.pallas import tpu as pltpu
from jax.sharding import PartitionSpec as P

XREACH = 64
RREACH = 8
LANES = 128
VMEM = pl.BlockSpec(memory_space=pltpu.VMEM)
SMEM = pl.BlockSpec(memory_space=pltpu.SMEM)
LIMIT = pltpu.CompilerParams(vmem_limit_bytes=32 * 1024 * 1024)


def pack_kernel(capacity, *refs):
    given, out_ref, (diag_ref, used_ref), held, sems = refs[:7], refs[7], refs[8:10], refs[10:17], refs[17]
    copies = [
        pltpu.make_async_copy(source, target, sems.at[index])
        for index, (source, target) in enumerate(zip(given, held, strict=True))
    ]
    for copy in copies:
        copy.start()
    tile_ref, cell_ref, id_ref, weight_ref, psi_ref, phi_ref, table_ref = held
    cells, epochs = psi_ref.shape[:2]
    tiles, width = out_ref.shape[0], psi_ref.shape[3]

    def clear(tile, carry):
        used_ref[tile] = 0
        out_ref[tile, 2 * capacity] = jnp.zeros(out_ref.shape[2:], jnp.float32)
        return carry

    lax.fori_loop(0, tiles, clear, 0)
    for copy in copies:
        copy.wait()

    source = lax.broadcasted_iota(jnp.int32, (width, width), 0)
    target = lax.broadcasted_iota(jnp.int32, (width, width), 1)
    for place in range(3):
        mask = source == target + (place - 1)
        for index in range(table_ref.shape[0]):
            row = jnp.sum(jnp.where(mask, table_ref[index], 0.0), axis=0, keepdims=True)
            diag_ref[index, place : place + 1, :] = row

    lane = lax.broadcasted_iota(jnp.int32, (1, LANES), 1)
    for block in range(cells):
        for epoch in range(epochs):
            tile = tile_ref[block, 0, epoch]
            slot = used_ref[tile]
            used_ref[tile] = slot + 1
            bands = diag_ref[id_ref[block, epoch]] * weight_ref[block, epoch]
            for kind, ref in enumerate((psi_ref, phi_ref)):
                values = ref[block, epoch]
                out_ref[tile, 2 * slot + kind] = (
                    values * bands[1:2]
                    + pltpu.roll(values, 1, 1) * bands[0:1]
                    + pltpu.roll(values, width - 1, 1) * bands[2:3]
                )
            place = (epoch * 2 * cells + cell_ref[block, epoch] + 1).astype(jnp.float32)
            note = out_ref[tile, 2 * capacity, 0:1, :]
            out_ref[tile, 2 * capacity, 0:1, :] = jnp.where(lane == slot, place, note)


def sum_kernel(capacity, cells, in_ref, sky_ref):
    for index in range(sky_ref.shape[0]):
        sky_ref[index] = jnp.zeros(sky_ref.shape[1:], jnp.float32)

    def one_source(source, carry):
        notes = in_ref[source, 2 * capacity].astype(jnp.int32)
        for slot in range(capacity):
            place = notes[0, slot] - 1
            there = place >= 0
            base = jnp.maximum(place, 0)
            for kind in range(2):
                value = jnp.where(there, in_ref[source, 2 * slot + kind], 0.0)
                sky_ref[base + kind * cells] = sky_ref[base + kind * cells] + value
        return carry

    lax.fori_loop(0, in_ref.shape[0], one_source, 0, unroll=16)


def shift_kernel(row_ref, col_ref, odd_ref, after_ref, row_out, col_out, odd_out):
    def one_epoch(epoch, carry):
        for vel in range(row_ref.shape[1]):
            row_out[epoch, vel] = row_ref[epoch, vel]
            col_out[epoch, vel] = col_ref[epoch, vel]
        return carry

    lax.fori_loop(0, row_ref.shape[0], one_epoch, 0)
    odd_out[0] = odd_ref[0]


def stack_kernel(cells, row_ref, col_ref, odd_ref, own_ref, far_ref, twin_ref, best_ref, wide_ref):
    epochs, vels = row_ref.shape
    rows = own_ref.shape[1]
    odd = odd_ref[0]
    twin_row = pl.multiple_of((1 - odd) * 2 * rows, rows)
    far_row = pl.multiple_of(odd * 2 * rows, rows)
    for epoch in range(epochs):
        for kind in range(2):
            zeros = jnp.zeros(wide_ref.shape[3:], jnp.float32)
            wide_ref[epoch, kind, 0] = zeros
            wide_ref[epoch, kind, cells + 1] = zeros
            for cell in range(cells):
                index = (epoch * 2 + kind) * cells + cell
                wide_ref[epoch, kind, cell + 1, rows : 2 * rows, :] = own_ref[index]
                wide_ref[epoch, kind, cell + 1, pl.ds(twin_row, rows), :] = twin_ref[index]
                wide_ref[epoch, kind, cell + 1, pl.ds(far_row, rows), :] = far_ref[index]
    lane = lax.broadcasted_iota(jnp.int32, (rows, LANES), 1)

    def one_velocity(vel, highest):
        sums = [[jnp.zeros((rows, LANES), jnp.float32) for _ in range(cells)] for _ in range(2)]
        for epoch in range(epochs):
            start_row = rows + row_ref[epoch, vel]
            start_col = LANES + col_ref[epoch, vel]
            first = lax.shift_right_logical(start_col, 7)
            shift = start_col & (LANES - 1)
            mask = lane >= shift
            turn = (LANES - shift) & (LANES - 1)
            for kind in range(2):
                parts = [
                    wide_ref[epoch, kind, first + step, pl.ds(start_row, rows), :]
                    for step in range(cells + 1)
                ]
                for cell in range(cells):
                    merged = jnp.where(mask, parts[cell], parts[cell + 1])
                    sums[kind][cell] = sums[kind][cell] + pltpu.roll(merged, turn, 1)
        return [
            jnp.maximum(highest[cell], sums[0][cell] / jnp.sqrt(jnp.maximum(sums[1][cell], 1.0)))
            for cell in range(cells)
        ]

    start = [jnp.full((rows, LANES), -jnp.inf, jnp.float32) for _ in range(cells)]
    highest = lax.fori_loop(0, vels, one_velocity, start, unroll=4)
    for cell in range(cells):
        best_ref[:, cell * LANES : (cell + 1) * LANES] = highest[cell]


def body(psi, phi, dest_tile, dest_cell, kernel_id, weight, kernels, row_offsets, col_offsets):
    tiles = lax.axis_size("tile")
    cells, epochs, rows, width = psi.shape
    capacity = max(2, 2 * cells * epochs // tiles)
    message = (tiles, 2 * capacity + 1, rows, width)
    given = (jnp.swapaxes(dest_tile, 1, 2), dest_cell, kernel_id, weight, psi, phi, kernels)
    outgoing = pl.pallas_call(
        functools.partial(pack_kernel, capacity),
        out_shape=jax.ShapeDtypeStruct(message, jnp.float32),
        in_specs=[pl.BlockSpec(memory_space=pl.ANY)] * 7,
        out_specs=VMEM,
        scratch_shapes=[
            pltpu.VMEM((kernels.shape[0], 3, width), jnp.float32),
            pltpu.SMEM((tiles,), jnp.int32),
        ]
        + [pltpu.SMEM(array.shape, array.dtype) for array in given[:4]]
        + [pltpu.VMEM(array.shape, array.dtype) for array in given[4:]]
        + [pltpu.SemaphoreType.DMA((7,))],
        compiler_params=pltpu.CompilerParams(vmem_limit_bytes=32 * 1024 * 1024),
        name="pack",
    )(*(pltpu.with_memory_space_constraint(array, pltpu.HBM) for array in given))
    incoming = lax.all_to_all(outgoing, "tile", split_axis=0, concat_axis=0, tiled=True)
    sky = pl.pallas_call(
        functools.partial(sum_kernel, capacity, cells),
        out_shape=jax.ShapeDtypeStruct((epochs * 2 * cells, rows, width), jnp.float32),
        in_specs=[VMEM],
        out_specs=VMEM,
        compiler_params=LIMIT,
        name="sum_slots",
    )(incoming)
    far = lax.ppermute(
        sky, "tile", [pair for i in range(1, tiles - 1, 2) for pair in ((i, i + 1), (i + 1, i))]
    )
    twin = lax.ppermute(sky, "tile", [(i, i ^ 1) for i in range(tiles)])
    odd = (lax.axis_index("tile") & 1).reshape(1)
    scalars = (row_offsets, col_offsets, odd)
    scalars = pl.pallas_call(
        shift_kernel,
        out_shape=[pltpu.SMEM(array.shape, array.dtype) for array in scalars],
        in_specs=[SMEM] * 3 + [pl.BlockSpec(memory_space=pl.ANY)],
        out_specs=[SMEM] * 3,
        compiler_params=LIMIT,
        name="shifts",
    )(*scalars, sky)
    return pl.pallas_call(
        functools.partial(stack_kernel, cells),
        out_shape=jax.ShapeDtypeStruct((rows, cells * width), jnp.float32),
        in_specs=[SMEM] * 3 + [VMEM] * 3,
        out_specs=VMEM,
        scratch_shapes=[pltpu.VMEM((epochs, 2, cells + 2, 3 * rows, width), jnp.float32)],
        compiler_params=LIMIT,
        name="stack",
    )(*scalars, sky, far, twin)


def solution(mesh):
    placed = (
        P(("field", "tile"), None, None, None),
        P(("field", "tile"), None, None, None),
        P(("field", "tile"), None, None),
        P(("field", "tile"), None),
        P(("field", "tile"), None),
        P(("field", "tile"), None),
        P(),
        P("field", None),
        P("field", None),
    )
    return jax.shard_map(
        body, mesh=mesh, in_specs=placed, out_specs=P(("field", "tile"), None), check_vma=False
    )
```

```python
import functools

import jax
import jax.numpy as jnp
from jax import lax
from jax.experimental import pallas as pl
from jax.experimental.pallas import tpu as pltpu
from jax.sharding import PartitionSpec as P

XREACH = 64
RREACH = 8
LANES = 128
GROUP = 24
VMEM = pl.BlockSpec(memory_space=pltpu.VMEM)
SMEM = pl.BlockSpec(memory_space=pltpu.SMEM)
LIMIT = pltpu.CompilerParams(vmem_limit_bytes=32 * 1024 * 1024)


def pack_kernel(capacity, *refs):
    given, out_ref, (diag_ref, note_ref, used_ref, spot_ref), held, sems = (
        refs[:7], refs[7], refs[8:12], refs[12:19], refs[19]
    )
    copies = [
        pltpu.make_async_copy(source, target, sems.at[index])
        for index, (source, target) in enumerate(zip(given, held, strict=True))
    ]
    for copy in copies[::-1]:
        copy.start()
    tile_ref, cell_ref, id_ref, weight_ref, psi_ref, phi_ref, table_ref = held
    cells, epochs = psi_ref.shape[:2]
    tiles, width = used_ref.shape[0], psi_ref.shape[3]
    stride = 2 * capacity + 1

    def clear(tile, carry):
        used_ref[tile] = 0
        note_ref[tile] = jnp.zeros(note_ref.shape[1:], jnp.float32)
        return carry

    lax.fori_loop(0, tiles, clear, 0, unroll=16)
    for copy in copies[:4]:
        copy.wait()

    lane = lax.broadcasted_iota(jnp.int32, (1, LANES), 1)
    for block in range(cells):
        for epoch in range(epochs):
            tile = tile_ref[block, 0, epoch]
            slot = used_ref[tile]
            used_ref[tile] = slot + 1
            spot_ref[block, epoch] = tile * stride + 2 * slot
            place = (epoch * 2 * cells + cell_ref[block, epoch] + 1).astype(jnp.float32)
            note_ref[tile] = jnp.where(lane == slot, place, note_ref[tile])
    for copy in copies[4:]:
        copy.wait()

    source = lax.broadcasted_iota(jnp.int32, (width, width), 0)
    target = lax.broadcasted_iota(jnp.int32, (width, width), 1)
    for place in range(3):
        mask = source == target + (place - 1)
        for index in range(table_ref.shape[0]):
            row = jnp.sum(jnp.where(mask, table_ref[index], 0.0), axis=0, keepdims=True)
            diag_ref[index, place : place + 1, :] = row

    def write_note(tile, carry):
        out_ref[tile * stride + 2 * capacity, 0:1, :] = note_ref[tile]
        return carry

    lax.fori_loop(0, tiles, write_note, 0, unroll=16)
    for block in range(cells):
        for epoch in range(epochs):
            spot = spot_ref[block, epoch]
            bands = diag_ref[id_ref[block, epoch]] * weight_ref[block, epoch]
            for kind, ref in enumerate((psi_ref, phi_ref)):
                values = ref[block, epoch]
                out_ref[spot + kind] = (
                    values * bands[1:2]
                    + pltpu.roll(values, 1, 1) * bands[0:1]
                    + pltpu.roll(values, width - 1, 1) * bands[2:3]
                )


def sum_kernel(capacity, cells, in_ref, sky_ref, *half_refs):
    for index in range(sky_ref.shape[0]):
        sky_ref[index] = jnp.zeros(sky_ref.shape[1:], jnp.float32)

    def one_source(source, carry):
        notes = in_ref[source, 2 * capacity].astype(jnp.int32)
        for slot in range(capacity):
            place = notes[0, slot] - 1
            there = place >= 0
            base = jnp.maximum(place, 0)
            for kind in range(2):
                value = jnp.where(there, in_ref[source, 2 * slot + kind], 0.0)
                sky_ref[base + kind * cells] = sky_ref[base + kind * cells] + value
        return carry

    lax.fori_loop(0, in_ref.shape[0], one_source, 0, unroll=16)
    for half, ref in enumerate(half_refs):
        for index in range(ref.shape[0]):
            ref[index] = sky_ref[half * ref.shape[0] + index]


def windows_at(ref, epoch, start_row, start_col, rows):
    first = lax.shift_right_logical(start_col, 7)
    shift = start_col & (LANES - 1)
    turn = (LANES - shift) & (LANES - 1)
    mask = lax.broadcasted_iota(jnp.int32, (rows, LANES), 1) >= shift
    windows = []
    for kind in range(2):
        parts = [
            ref[epoch, kind, first + step, pl.ds(start_row, rows), :]
            for step in range(ref.shape[2] - 1)
        ]
        windows.append(
            [
                pltpu.roll(jnp.where(mask, parts[cell], parts[cell + 1]), turn, 1)
                for cell in range(len(parts) - 1)
            ]
        )
    return windows


def clear_sides(ref, epoch, kind):
    for side in (0, ref.shape[2] - 1):
        ref[epoch, kind, side] = jnp.zeros(ref.shape[3:], jnp.float32)


def near_kernel(
    cells, group, row_ref, col_ref, odd_ref, own_ref, low_ref, high_ref, sums_ref, list_ref, count_ref, wide_ref
):
    epochs, vels = row_ref.shape
    rows = own_ref.shape[1]
    odd = odd_ref[0]
    twin_row = pl.multiple_of((1 - odd) * 2 * rows, rows)
    far_row = pl.multiple_of(odd * 2 * rows, rows)
    for epoch in range(epochs):
        for kind in range(2):
            clear_sides(wide_ref, epoch, kind)
            for cell in range(cells):
                index = (epoch * 2 + kind) * cells + cell
                wide_ref[epoch, kind, cell + 1, rows : 2 * rows, :] = own_ref[index]
                half, place = divmod(index, low_ref.shape[0])
                wide_ref[epoch, kind, cell + 1, pl.ds(twin_row, rows), :] = (low_ref, high_ref)[half][place]
                wide_ref[epoch, kind, cell + 1, pl.ds(far_row, rows), :] = jnp.zeros(
                    (rows, LANES), jnp.float32
                )

    def one_velocity(vel, count):
        sums = [[jnp.zeros((rows, LANES), jnp.float32) for _ in range(cells)] for _ in range(2)]
        for epoch in range(epochs):
            row = row_ref[epoch, vel]
            start_col = LANES + col_ref[epoch, vel]
            windows = windows_at(wide_ref, epoch, rows + row, start_col, rows)
            for kind in range(2):
                for cell in range(cells):
                    sums[kind][cell] = sums[kind][cell] + windows[kind][cell]
            reach = row * (2 * odd - 1)
            start_row = row + (1 - odd) * rows
            list_ref[count] = (vel << 24) | (epoch << 16) | (start_row << 10) | start_col
            count = count + jnp.where(reach > 0, 1, 0)
        for kind in range(2):
            for cell in range(cells):
                sums_ref[vel, kind, cell] = sums[kind][cell]
        return count

    count = lax.fori_loop(0, vels, one_velocity, jnp.int32(0), unroll=4)
    for index in range(group):
        list_ref[count + index] = (((1 - odd) * rows) << 10) | LANES
    count_ref[0] = count
    count_ref[1] = odd


def far_kernel(cells, group, list_ref, count_ref, far_ref, given_ref, sums_ref, best_ref, wide_ref):
    vels = sums_ref.shape[0]
    rows = far_ref.shape[1]
    epochs = wide_ref.shape[0]
    far_row = pl.multiple_of(count_ref[1] * rows, rows)
    zero_row = pl.multiple_of((1 - count_ref[1]) * rows, rows)
    for epoch in range(epochs):
        for kind in range(2):
            clear_sides(wide_ref, epoch, kind)
            for cell in range(cells):
                index = (epoch * 2 + kind) * cells + cell
                wide_ref[epoch, kind, cell + 1, pl.ds(far_row, rows), :] = far_ref[index]
                wide_ref[epoch, kind, cell + 1, pl.ds(zero_row, rows), :] = jnp.zeros(
                    (rows, LANES), jnp.float32
                )

    def one_group(turn, carry):
        found = []
        for index in range(group):
            code = list_ref[turn * group + index]
            start_col = code & 1023
            start_row = (code >> 10) & 63
            epoch = (code >> 16) & 255
            found.append((code >> 24, windows_at(wide_ref, epoch, start_row, start_col, rows)))
        for vel, windows in found:
            for kind in range(2):
                for cell in range(cells):
                    sums_ref[vel, kind, cell] = sums_ref[vel, kind, cell] + windows[kind][cell]
        return carry

    lax.fori_loop(0, lax.div(count_ref[0] + group - 1, group), one_group, 0)
    highest = [jnp.full((rows, LANES), -jnp.inf, jnp.float32) for _ in range(cells)]
    for vel in range(vels):
        for cell in range(cells):
            scale = lax.rsqrt(jnp.maximum(sums_ref[vel, 1, cell], 1.0))
            highest[cell] = jnp.maximum(highest[cell], sums_ref[vel, 0, cell] * scale)
    for cell in range(cells):
        best_ref[:, cell * LANES : (cell + 1) * LANES] = highest[cell]


def body(psi, phi, dest_tile, dest_cell, kernel_id, weight, kernels, row_offsets, col_offsets):
    tiles = lax.axis_size("tile")
    cells, epochs, rows, width = psi.shape
    capacity = max(2, 2 * cells * epochs // tiles)
    message = (tiles * (2 * capacity + 1), rows, width)
    given = (jnp.swapaxes(dest_tile, 1, 2), dest_cell, kernel_id, weight, psi, phi, kernels)
    outgoing = pl.pallas_call(
        functools.partial(pack_kernel, capacity),
        out_shape=jax.ShapeDtypeStruct(message, jnp.float32),
        in_specs=[pl.BlockSpec(memory_space=pl.ANY)] * 7,
        out_specs=VMEM,
        scratch_shapes=[
            pltpu.VMEM((kernels.shape[0], 3, width), jnp.float32),
            pltpu.VMEM((tiles, 1, LANES), jnp.float32),
            pltpu.SMEM((tiles,), jnp.int32),
            pltpu.SMEM((cells, epochs), jnp.int32),
        ]
        + [pltpu.SMEM(array.shape, array.dtype) for array in given[:4]]
        + [pltpu.VMEM(array.shape, array.dtype) for array in given[4:]]
        + [pltpu.SemaphoreType.DMA((7,))],
        compiler_params=pltpu.CompilerParams(vmem_limit_bytes=32 * 1024 * 1024),
        name="pack",
    )(*(pltpu.with_memory_space_constraint(array, pltpu.HBM) for array in given))
    outgoing = outgoing.reshape(tiles, 2 * capacity + 1, rows, width)
    incoming = lax.all_to_all(outgoing, "tile", split_axis=0, concat_axis=0, tiled=True)
    sky, *halves = pl.pallas_call(
        functools.partial(sum_kernel, capacity, cells),
        out_shape=[
            jax.ShapeDtypeStruct((epochs * 2 * cells // parts, rows, width), jnp.float32)
            for parts in (1, 2, 2)
        ],
        in_specs=[VMEM],
        out_specs=[VMEM] * 3,
        compiler_params=LIMIT,
        name="sum_slots",
    )(incoming)
    far = lax.ppermute(
        sky, "tile", [pair for i in range(1, tiles - 1, 2) for pair in ((i, i + 1), (i + 1, i))]
    )
    twins = [lax.ppermute(half, "tile", [(i, i ^ 1) for i in range(tiles)]) for half in halves]
    odd = (lax.axis_index("tile") & 1).reshape(1)
    vels = row_offsets.shape[1]
    sums_shape = jax.ShapeDtypeStruct((vels, 2, cells, rows, width), jnp.float32)
    sums, listed, count = pl.pallas_call(
        functools.partial(near_kernel, cells, GROUP),
        out_shape=[
            sums_shape,
            pltpu.SMEM((vels * epochs + GROUP,), jnp.int32),
            pltpu.SMEM((2,), jnp.int32),
        ],
        in_specs=[SMEM] * 3 + [VMEM] * 3,
        out_specs=[VMEM, SMEM, SMEM],
        scratch_shapes=[pltpu.VMEM((epochs, 2, cells + 2, 3 * rows, width), jnp.float32)],
        compiler_params=LIMIT,
        name="stack_near",
    )(row_offsets, col_offsets, odd, sky, *twins)
    _, best = pl.pallas_call(
        functools.partial(far_kernel, cells, GROUP),
        out_shape=[sums_shape, jax.ShapeDtypeStruct((rows, cells * width), jnp.float32)],
        in_specs=[SMEM] * 2 + [VMEM] * 2,
        out_specs=[VMEM, VMEM],
        input_output_aliases={3: 0},
        scratch_shapes=[pltpu.VMEM((epochs, 2, cells + 2, 2 * rows, width), jnp.float32)],
        compiler_params=LIMIT,
        name="stack_far",
    )(listed, count, far, sums)
    return best


def solution(mesh):
    placed = (
        P(("field", "tile"), None, None, None),
        P(("field", "tile"), None, None, None),
        P(("field", "tile"), None, None),
        P(("field", "tile"), None),
        P(("field", "tile"), None),
        P(("field", "tile"), None),
        P(),
        P("field", None),
        P("field", None),
    )
    return jax.shard_map(
        body, mesh=mesh, in_specs=placed, out_specs=P(("field", "tile"), None), check_vma=False
    )
```

```python
import functools

import jax
import jax.numpy as jnp
from jax import lax
from jax.experimental import pallas as pl
from jax.experimental.pallas import tpu as pltpu
from jax.sharding import PartitionSpec as P

XREACH = 64
RREACH = 8
LANES = 128
GROUP = 24
VMEM = pl.BlockSpec(memory_space=pltpu.VMEM)
SMEM = pl.BlockSpec(memory_space=pltpu.SMEM)
LIMIT = pltpu.CompilerParams(vmem_limit_bytes=32 * 1024 * 1024)


def pack_kernel(capacity, *refs):
    given, out_ref, (diag_ref, note_ref, used_ref, spot_ref), held, sems = (
        refs[:7], refs[7], refs[8:12], refs[12:19], refs[19]
    )
    copies = [
        pltpu.make_async_copy(source, target, sems.at[index])
        for index, (source, target) in enumerate(zip(given, held, strict=True))
    ]
    for copy in copies[::-1]:
        copy.start()
    tile_ref, cell_ref, id_ref, weight_ref, psi_ref, phi_ref, table_ref = held
    cells, epochs = psi_ref.shape[:2]
    tiles, width = used_ref.shape[0], psi_ref.shape[3]
    rows = psi_ref.shape[2]
    stride = 2 * capacity * rows + 1

    def clear(tile, carry):
        used_ref[tile] = 0
        note_ref[tile] = jnp.zeros(note_ref.shape[1:], jnp.float32)
        return carry

    lax.fori_loop(0, tiles, clear, 0, unroll=16)
    for copy in copies[:4]:
        copy.wait()

    lane = lax.broadcasted_iota(jnp.int32, (1, LANES), 1)
    for block in range(cells):
        for epoch in range(epochs):
            tile = tile_ref[block, 0, epoch]
            slot = used_ref[tile]
            used_ref[tile] = slot + 1
            spot_ref[block, epoch] = tile * stride + 2 * rows * slot
            place = (epoch * 2 * cells + cell_ref[block, epoch] + 1).astype(jnp.float32)
            note_ref[tile] = jnp.where(lane == slot, place, note_ref[tile])
    for copy in copies[4:]:
        copy.wait()

    source = lax.broadcasted_iota(jnp.int32, (width, width), 0)
    target = lax.broadcasted_iota(jnp.int32, (width, width), 1)
    for place in range(3):
        mask = source == target + (place - 1)
        for index in range(table_ref.shape[0]):
            row = jnp.sum(jnp.where(mask, table_ref[index], 0.0), axis=0, keepdims=True)
            diag_ref[index, place : place + 1, :] = row

    def write_note(tile, carry):
        out_ref[pl.ds(tile * stride + stride - 1, 1), :] = note_ref[tile]
        return carry

    lax.fori_loop(0, tiles, write_note, 0, unroll=16)
    for block in range(cells):
        for epoch in range(epochs):
            spot = spot_ref[block, epoch]
            bands = diag_ref[id_ref[block, epoch]] * weight_ref[block, epoch]
            for kind, ref in enumerate((psi_ref, phi_ref)):
                values = ref[block, epoch]
                out_ref[pl.ds(spot + kind * rows, rows), :] = (
                    values * bands[1:2]
                    + pltpu.roll(values, 1, 1) * bands[0:1]
                    + pltpu.roll(values, width - 1, 1) * bands[2:3]
                )


def sum_kernel(capacity, cells, in_ref, sky_ref, *half_refs):
    rows = sky_ref.shape[1]
    stride = 2 * capacity * rows + 1
    for index in range(sky_ref.shape[0]):
        sky_ref[index] = jnp.zeros(sky_ref.shape[1:], jnp.float32)

    def one_source(source, carry):
        first = source * stride
        notes = in_ref[pl.ds(first + stride - 1, 1), :].astype(jnp.int32)
        for slot in range(capacity):
            place = notes[0, slot] - 1
            there = place >= 0
            base = jnp.maximum(place, 0)
            for kind in range(2):
                value = in_ref[pl.ds(first + (2 * slot + kind) * rows, rows), :]
                value = jnp.where(there, value, 0.0)
                sky_ref[base + kind * cells] = sky_ref[base + kind * cells] + value
        return carry

    lax.fori_loop(0, in_ref.shape[0] // stride, one_source, 0, unroll=16)
    for half, ref in enumerate(half_refs):
        for index in range(ref.shape[0]):
            ref[index] = sky_ref[half * ref.shape[0] + index]


def windows_at(ref, epoch, start_row, start_col, rows):
    first = lax.shift_right_logical(start_col, 7)
    shift = start_col & (LANES - 1)
    turn = (LANES - shift) & (LANES - 1)
    mask = lax.broadcasted_iota(jnp.int32, (rows, LANES), 1) >= shift
    windows = []
    for kind in range(2):
        parts = [
            ref[epoch, kind, first + step, pl.ds(start_row, rows), :]
            for step in range(ref.shape[2] - 1)
        ]
        windows.append(
            [
                pltpu.roll(jnp.where(mask, parts[cell], parts[cell + 1]), turn, 1)
                for cell in range(len(parts) - 1)
            ]
        )
    return windows


def clear_sides(ref, epoch, kind):
    for side in (0, ref.shape[2] - 1):
        ref[epoch, kind, side] = jnp.zeros(ref.shape[3:], jnp.float32)


def near_kernel(
    cells, group, row_ref, col_ref, odd_ref, own_ref, low_ref, high_ref, sums_ref, list_ref, count_ref, wide_ref
):
    epochs, vels = row_ref.shape
    rows = own_ref.shape[1]
    odd = odd_ref[0]
    twin_row = pl.multiple_of((1 - odd) * 2 * rows, rows)
    far_row = pl.multiple_of(odd * 2 * rows, rows)
    for epoch in range(epochs):
        for kind in range(2):
            clear_sides(wide_ref, epoch, kind)
            for cell in range(cells):
                index = (epoch * 2 + kind) * cells + cell
                wide_ref[epoch, kind, cell + 1, rows : 2 * rows, :] = own_ref[index]
                half, place = divmod(index, low_ref.shape[0])
                wide_ref[epoch, kind, cell + 1, pl.ds(twin_row, rows), :] = (low_ref, high_ref)[half][place]
                wide_ref[epoch, kind, cell + 1, pl.ds(far_row, rows), :] = jnp.zeros(
                    (rows, LANES), jnp.float32
                )

    def one_velocity(vel, count):
        sums = [[jnp.zeros((rows, LANES), jnp.float32) for _ in range(cells)] for _ in range(2)]
        for epoch in range(epochs):
            row = row_ref[epoch, vel]
            start_col = LANES + col_ref[epoch, vel]
            windows = windows_at(wide_ref, epoch, rows + row, start_col, rows)
            for kind in range(2):
                for cell in range(cells):
                    sums[kind][cell] = sums[kind][cell] + windows[kind][cell]
            reach = row * (2 * odd - 1)
            start_row = row + (1 - odd) * rows
            list_ref[count] = (vel << 24) | (epoch << 16) | (start_row << 10) | start_col
            count = count + jnp.where(reach > 0, 1, 0)
        for kind in range(2):
            for cell in range(cells):
                sums_ref[vel, kind, cell] = sums[kind][cell]
        return count

    count = lax.fori_loop(0, vels, one_velocity, jnp.int32(0), unroll=4)
    for index in range(group):
        list_ref[count + index] = (((1 - odd) * rows) << 10) | LANES
    count_ref[0] = count
    count_ref[1] = odd


def far_kernel(cells, group, list_ref, count_ref, far_ref, given_ref, sums_ref, best_ref, wide_ref):
    vels = sums_ref.shape[0]
    rows = far_ref.shape[1]
    epochs = wide_ref.shape[0]
    far_row = pl.multiple_of(count_ref[1] * rows, rows)
    zero_row = pl.multiple_of((1 - count_ref[1]) * rows, rows)
    for epoch in range(epochs):
        for kind in range(2):
            clear_sides(wide_ref, epoch, kind)
            for cell in range(cells):
                index = (epoch * 2 + kind) * cells + cell
                wide_ref[epoch, kind, cell + 1, pl.ds(far_row, rows), :] = far_ref[index]
                wide_ref[epoch, kind, cell + 1, pl.ds(zero_row, rows), :] = jnp.zeros(
                    (rows, LANES), jnp.float32
                )

    def one_group(turn, carry):
        found = []
        for index in range(group):
            code = list_ref[turn * group + index]
            start_col = code & 1023
            start_row = (code >> 10) & 63
            epoch = (code >> 16) & 255
            found.append((code >> 24, windows_at(wide_ref, epoch, start_row, start_col, rows)))
        for vel, windows in found:
            for kind in range(2):
                for cell in range(cells):
                    sums_ref[vel, kind, cell] = sums_ref[vel, kind, cell] + windows[kind][cell]
        return carry

    lax.fori_loop(0, lax.div(count_ref[0] + group - 1, group), one_group, 0)
    highest = [jnp.full((rows, LANES), -jnp.inf, jnp.float32) for _ in range(cells)]
    for vel in range(vels):
        for cell in range(cells):
            scale = lax.rsqrt(jnp.maximum(sums_ref[vel, 1, cell], 1.0))
            highest[cell] = jnp.maximum(highest[cell], sums_ref[vel, 0, cell] * scale)
    for cell in range(cells):
        best_ref[:, cell * LANES : (cell + 1) * LANES] = highest[cell]


def body(psi, phi, dest_tile, dest_cell, kernel_id, weight, kernels, row_offsets, col_offsets):
    tiles = lax.axis_size("tile")
    cells, epochs, rows, width = psi.shape
    capacity = max(2, 2 * cells * epochs // tiles)
    stride = 2 * capacity * rows + 1
    message = (tiles * stride, width)
    given = (jnp.swapaxes(dest_tile, 1, 2), dest_cell, kernel_id, weight, psi, phi, kernels)
    outgoing = pl.pallas_call(
        functools.partial(pack_kernel, capacity),
        out_shape=jax.ShapeDtypeStruct(message, jnp.float32),
        in_specs=[pl.BlockSpec(memory_space=pl.ANY)] * 7,
        out_specs=VMEM,
        scratch_shapes=[
            pltpu.VMEM((kernels.shape[0], 3, width), jnp.float32),
            pltpu.VMEM((tiles, 1, LANES), jnp.float32),
            pltpu.SMEM((tiles,), jnp.int32),
            pltpu.SMEM((cells, epochs), jnp.int32),
        ]
        + [pltpu.SMEM(array.shape, array.dtype) for array in given[:4]]
        + [pltpu.VMEM(array.shape, array.dtype) for array in given[4:]]
        + [pltpu.SemaphoreType.DMA((7,))],
        compiler_params=pltpu.CompilerParams(vmem_limit_bytes=32 * 1024 * 1024),
        name="pack",
    )(*(pltpu.with_memory_space_constraint(array, pltpu.HBM) for array in given))
    outgoing = outgoing.reshape(tiles, stride, 1, width)
    incoming = lax.all_to_all(outgoing, "tile", split_axis=0, concat_axis=0, tiled=True)
    incoming = incoming.reshape(message)
    sky, *halves = pl.pallas_call(
        functools.partial(sum_kernel, capacity, cells),
        out_shape=[
            jax.ShapeDtypeStruct((epochs * 2 * cells // parts, rows, width), jnp.float32)
            for parts in (1, 2, 2)
        ],
        in_specs=[VMEM],
        out_specs=[VMEM] * 3,
        compiler_params=LIMIT,
        name="sum_slots",
    )(incoming)
    far = lax.ppermute(
        sky, "tile", [pair for i in range(1, tiles - 1, 2) for pair in ((i, i + 1), (i + 1, i))]
    )
    twins = [lax.ppermute(half, "tile", [(i, i ^ 1) for i in range(tiles)]) for half in halves]
    odd = (lax.axis_index("tile") & 1).reshape(1)
    vels = row_offsets.shape[1]
    sums_shape = jax.ShapeDtypeStruct((vels, 2, cells, rows, width), jnp.float32)
    sums, listed, count = pl.pallas_call(
        functools.partial(near_kernel, cells, GROUP),
        out_shape=[
            sums_shape,
            pltpu.SMEM((vels * epochs + GROUP,), jnp.int32),
            pltpu.SMEM((2,), jnp.int32),
        ],
        in_specs=[SMEM] * 3 + [VMEM] * 3,
        out_specs=[VMEM, SMEM, SMEM],
        scratch_shapes=[pltpu.VMEM((epochs, 2, cells + 2, 3 * rows, width), jnp.float32)],
        compiler_params=LIMIT,
        name="stack_near",
    )(row_offsets, col_offsets, odd, sky, *twins)
    _, best = pl.pallas_call(
        functools.partial(far_kernel, cells, GROUP),
        out_shape=[sums_shape, jax.ShapeDtypeStruct((rows, cells * width), jnp.float32)],
        in_specs=[SMEM] * 2 + [VMEM] * 2,
        out_specs=[VMEM, VMEM],
        input_output_aliases={3: 0},
        scratch_shapes=[pltpu.VMEM((epochs, 2, cells + 2, 2 * rows, width), jnp.float32)],
        compiler_params=LIMIT,
        name="stack_far",
    )(listed, count, far, sums)
    return best


def solution(mesh):
    placed = (
        P(("field", "tile"), None, None, None),
        P(("field", "tile"), None, None, None),
        P(("field", "tile"), None, None),
        P(("field", "tile"), None),
        P(("field", "tile"), None),
        P(("field", "tile"), None),
        P(),
        P("field", None),
        P("field", None),
    )
    return jax.shard_map(
        body, mesh=mesh, in_specs=placed, out_specs=P(("field", "tile"), None), check_vma=False
    )
```

```python
import functools

import jax
import jax.numpy as jnp
from jax import lax
from jax.experimental import pallas as pl
from jax.experimental.pallas import tpu as pltpu
from jax.sharding import PartitionSpec as P

XREACH = 64
RREACH = 8
LANES = 128
GROUP = 24
VMEM = pl.BlockSpec(memory_space=pltpu.VMEM)
SMEM = pl.BlockSpec(memory_space=pltpu.SMEM)
LIMIT = pltpu.CompilerParams(vmem_limit_bytes=32 * 1024 * 1024)


def pack_kernel(capacity, *refs):
    given, out_ref, (diag_ref, note_ref, used_ref, spot_ref), held, sems = (
        refs[:7], refs[7], refs[8:12], refs[12:19], refs[19]
    )
    copies = [
        pltpu.make_async_copy(source, target, sems.at[index])
        for index, (source, target) in enumerate(zip(given, held, strict=True))
    ]
    for copy in copies[::-1]:
        copy.start()
    tile_ref, cell_ref, id_ref, weight_ref, psi_ref, phi_ref, table_ref = held
    cells, epochs = psi_ref.shape[:2]
    tiles, width = used_ref.shape[0], psi_ref.shape[3]
    rows = psi_ref.shape[2]
    stride = 2 * capacity * rows + 1

    def clear(tile, carry):
        used_ref[tile] = 0
        note_ref[tile] = jnp.zeros(note_ref.shape[1:], jnp.float32)
        return carry

    lax.fori_loop(0, tiles, clear, 0, unroll=16)
    for copy in copies[:4]:
        copy.wait()

    lane = lax.broadcasted_iota(jnp.int32, (1, LANES), 1)
    for block in range(cells):
        for epoch in range(epochs):
            tile = tile_ref[block, 0, epoch]
            slot = used_ref[tile]
            used_ref[tile] = slot + 1
            spot_ref[block, epoch] = tile * stride + 2 * rows * slot
            place = (epoch * 2 * cells + cell_ref[block, epoch] + 1).astype(jnp.float32)
            note_ref[tile] = jnp.where(lane == slot, place, note_ref[tile])
    for copy in copies[4:]:
        copy.wait()

    source = lax.broadcasted_iota(jnp.int32, (width, width), 0)
    target = lax.broadcasted_iota(jnp.int32, (width, width), 1)
    for place in range(3):
        mask = source == target + (place - 1)
        for index in range(table_ref.shape[0]):
            row = jnp.sum(jnp.where(mask, table_ref[index], 0.0), axis=0, keepdims=True)
            diag_ref[index, place : place + 1, :] = row

    def write_note(tile, carry):
        out_ref[pl.ds(tile * stride + stride - 1, 1), :] = note_ref[tile]
        return carry

    lax.fori_loop(0, tiles, write_note, 0, unroll=16)
    for block in range(cells):
        for epoch in range(epochs):
            spot = spot_ref[block, epoch]
            bands = diag_ref[id_ref[block, epoch]] * weight_ref[block, epoch]
            for kind, ref in enumerate((psi_ref, phi_ref)):
                values = ref[block, epoch]
                out_ref[pl.ds(spot + kind * rows, rows), :] = (
                    values * bands[1:2]
                    + pltpu.roll(values, 1, 1) * bands[0:1]
                    + pltpu.roll(values, width - 1, 1) * bands[2:3]
                )


def sum_kernel(capacity, cells, in_ref, sky_ref, *half_refs):
    rows = sky_ref.shape[1]
    stride = 2 * capacity * rows + 1
    for index in range(sky_ref.shape[0]):
        sky_ref[index] = jnp.zeros(sky_ref.shape[1:], jnp.float32)

    def one_source(source, carry):
        first = source * stride
        notes = in_ref[pl.ds(first + stride - 1, 1), :].astype(jnp.int32)
        for slot in range(capacity):
            place = notes[0, slot] - 1
            there = place >= 0
            base = jnp.maximum(place, 0)
            for kind in range(2):
                value = in_ref[pl.ds(first + (2 * slot + kind) * rows, rows), :]
                value = jnp.where(there, value, 0.0)
                sky_ref[base + kind * cells] = sky_ref[base + kind * cells] + value
        return carry

    lax.fori_loop(0, in_ref.shape[0] // stride, one_source, 0, unroll=16)
    for half, ref in enumerate(half_refs):
        for index in range(ref.shape[0]):
            ref[index] = sky_ref[half * ref.shape[0] + index]


def windows_at(ref, epoch, start_row, start_col, rows):
    first = lax.shift_right_logical(start_col, 7)
    shift = start_col & (LANES - 1)
    turn = (LANES - shift) & (LANES - 1)
    mask = lax.broadcasted_iota(jnp.int32, (rows, LANES), 1) >= shift
    windows = []
    for kind in range(2):
        parts = [
            ref[epoch, kind, first + step, pl.ds(start_row, rows), :]
            for step in range(ref.shape[2] - 1)
        ]
        windows.append(
            [
                pltpu.roll(jnp.where(mask, parts[cell], parts[cell + 1]), turn, 1)
                for cell in range(len(parts) - 1)
            ]
        )
    return windows


def clear_sides(ref, epoch, kind):
    for side in (0, ref.shape[2] - 1):
        ref[epoch, kind, side] = jnp.zeros(ref.shape[3:], jnp.float32)


def near_kernel(
    cells, tiles, group, row_ref, col_ref, me_ref, own_ref, low_ref, high_ref, sums_ref, list_ref, count_ref, wide_ref
):
    epochs, vels = row_ref.shape
    rows = own_ref.shape[1]
    odd = me_ref[0] & 1
    towards = jnp.where((me_ref[0] == 0) | (me_ref[0] == tiles - 1), 0, 2 * odd - 1)
    twin_row = pl.multiple_of((1 - odd) * 2 * rows, rows)
    far_row = pl.multiple_of(odd * 2 * rows, rows)
    for epoch in range(epochs):
        for kind in range(2):
            clear_sides(wide_ref, epoch, kind)
            for cell in range(cells):
                index = (epoch * 2 + kind) * cells + cell
                wide_ref[epoch, kind, cell + 1, rows : 2 * rows, :] = own_ref[index]
                half, place = divmod(index, low_ref.shape[0])
                wide_ref[epoch, kind, cell + 1, pl.ds(twin_row, rows), :] = (low_ref, high_ref)[half][place]
                wide_ref[epoch, kind, cell + 1, pl.ds(far_row, rows), :] = jnp.zeros(
                    (rows, LANES), jnp.float32
                )

    def one_velocity(vel, count):
        sums = [[jnp.zeros((rows, LANES), jnp.float32) for _ in range(cells)] for _ in range(2)]
        for epoch in range(epochs):
            row = row_ref[epoch, vel]
            start_col = LANES + col_ref[epoch, vel]
            windows = windows_at(wide_ref, epoch, rows + row, start_col, rows)
            for kind in range(2):
                for cell in range(cells):
                    sums[kind][cell] = sums[kind][cell] + windows[kind][cell]
            reach = row * towards
            start_row = row + (1 - odd) * rows
            list_ref[count] = (vel << 24) | (epoch << 16) | (start_row << 10) | start_col
            count = count + jnp.where(reach > 0, 1, 0)
        for kind in range(2):
            for cell in range(cells):
                sums_ref[vel, kind, cell] = sums[kind][cell]
        return count

    count = lax.fori_loop(0, vels, one_velocity, jnp.int32(0), unroll=4)
    for index in range(group):
        list_ref[count + index] = (((1 - odd) * rows) << 10) | LANES
    count_ref[0] = count
    count_ref[1] = odd


def far_kernel(cells, group, list_ref, count_ref, far_ref, given_ref, sums_ref, best_ref, wide_ref):
    vels = sums_ref.shape[0]
    rows = far_ref.shape[1]
    epochs = wide_ref.shape[0]
    far_row = pl.multiple_of(count_ref[1] * rows, rows)
    zero_row = pl.multiple_of((1 - count_ref[1]) * rows, rows)
    for epoch in range(epochs):
        for kind in range(2):
            clear_sides(wide_ref, epoch, kind)
            for cell in range(cells):
                index = (epoch * 2 + kind) * cells + cell
                wide_ref[epoch, kind, cell + 1, pl.ds(far_row, rows), :] = far_ref[index]
                wide_ref[epoch, kind, cell + 1, pl.ds(zero_row, rows), :] = jnp.zeros(
                    (rows, LANES), jnp.float32
                )

    def one_group(turn, carry):
        found = []
        for index in range(group):
            code = list_ref[turn * group + index]
            start_col = code & 1023
            start_row = (code >> 10) & 63
            epoch = (code >> 16) & 255
            found.append((code >> 24, windows_at(wide_ref, epoch, start_row, start_col, rows)))
        for vel, windows in found:
            for kind in range(2):
                for cell in range(cells):
                    sums_ref[vel, kind, cell] = sums_ref[vel, kind, cell] + windows[kind][cell]
        return carry

    lax.fori_loop(0, lax.div(count_ref[0] + group - 1, group), one_group, 0)
    highest = [jnp.full((rows, LANES), -jnp.inf, jnp.float32) for _ in range(cells)]
    for vel in range(vels):
        for cell in range(cells):
            scale = lax.rsqrt(jnp.maximum(sums_ref[vel, 1, cell], 1.0))
            highest[cell] = jnp.maximum(highest[cell], sums_ref[vel, 0, cell] * scale)
    for cell in range(cells):
        best_ref[:, cell * LANES : (cell + 1) * LANES] = highest[cell]


def body(psi, phi, dest_tile, dest_cell, kernel_id, weight, kernels, row_offsets, col_offsets):
    tiles = lax.axis_size("tile")
    cells, epochs, rows, width = psi.shape
    capacity = max(2, 2 * cells * epochs // tiles)
    stride = 2 * capacity * rows + 1
    message = (tiles * stride, width)
    given = (jnp.swapaxes(dest_tile, 1, 2), dest_cell, kernel_id, weight, psi, phi, kernels)
    outgoing = pl.pallas_call(
        functools.partial(pack_kernel, capacity),
        out_shape=jax.ShapeDtypeStruct(message, jnp.float32),
        in_specs=[pl.BlockSpec(memory_space=pl.ANY)] * 7,
        out_specs=VMEM,
        scratch_shapes=[
            pltpu.VMEM((kernels.shape[0], 3, width), jnp.float32),
            pltpu.VMEM((tiles, 1, LANES), jnp.float32),
            pltpu.SMEM((tiles,), jnp.int32),
            pltpu.SMEM((cells, epochs), jnp.int32),
        ]
        + [pltpu.SMEM(array.shape, array.dtype) for array in given[:4]]
        + [pltpu.VMEM(array.shape, array.dtype) for array in given[4:]]
        + [pltpu.SemaphoreType.DMA((7,))],
        compiler_params=pltpu.CompilerParams(vmem_limit_bytes=32 * 1024 * 1024),
        name="pack",
    )(*(pltpu.with_memory_space_constraint(array, pltpu.HBM) for array in given))
    outgoing = outgoing.reshape(tiles, stride, 1, width)
    incoming = lax.all_to_all(outgoing, "tile", split_axis=0, concat_axis=0, tiled=True)
    incoming = incoming.reshape(message)
    sky, *halves = pl.pallas_call(
        functools.partial(sum_kernel, capacity, cells),
        out_shape=[
            jax.ShapeDtypeStruct((epochs * 2 * cells // parts, rows, width), jnp.float32)
            for parts in (1, 2, 2)
        ],
        in_specs=[VMEM],
        out_specs=[VMEM] * 3,
        compiler_params=LIMIT,
        name="sum_slots",
    )(incoming)
    fields = lax.axis_size("field")
    pairs = [(f * tiles + i, f * tiles + i + 1) for f in range(fields) for i in range(1, tiles - 1, 2)]
    pairs += [
        (f * tiles + i, (f + 1) * tiles + i) for f in range(0, fields - 1, 2) for i in (0, tiles - 1)
    ]
    far = lax.ppermute(
        sky, ("field", "tile"), [way for a, b in pairs for way in ((a, b), (b, a))]
    )
    twins = [lax.ppermute(half, "tile", [(i, i ^ 1) for i in range(tiles)]) for half in halves]
    me = lax.axis_index("tile").reshape(1)
    vels = row_offsets.shape[1]
    sums_shape = jax.ShapeDtypeStruct((vels, 2, cells, rows, width), jnp.float32)
    sums, listed, count = pl.pallas_call(
        functools.partial(near_kernel, cells, tiles, GROUP),
        out_shape=[
            sums_shape,
            pltpu.SMEM((vels * epochs + GROUP,), jnp.int32),
            pltpu.SMEM((2,), jnp.int32),
        ],
        in_specs=[SMEM] * 3 + [VMEM] * 3,
        out_specs=[VMEM, SMEM, SMEM],
        scratch_shapes=[pltpu.VMEM((epochs, 2, cells + 2, 3 * rows, width), jnp.float32)],
        compiler_params=LIMIT,
        name="stack_near",
    )(row_offsets, col_offsets, me, sky, *twins)
    _, best = pl.pallas_call(
        functools.partial(far_kernel, cells, GROUP),
        out_shape=[sums_shape, jax.ShapeDtypeStruct((rows, cells * width), jnp.float32)],
        in_specs=[SMEM] * 2 + [VMEM] * 2,
        out_specs=[VMEM, VMEM],
        input_output_aliases={3: 0},
        scratch_shapes=[pltpu.VMEM((epochs, 2, cells + 2, 2 * rows, width), jnp.float32)],
        compiler_params=LIMIT,
        name="stack_far",
    )(listed, count, far, sums)
    return best


def solution(mesh):
    placed = (
        P(("field", "tile"), None, None, None),
        P(("field", "tile"), None, None, None),
        P(("field", "tile"), None, None),
        P(("field", "tile"), None),
        P(("field", "tile"), None),
        P(("field", "tile"), None),
        P(),
        P("field", None),
        P("field", None),
    )
    return jax.shard_map(
        body, mesh=mesh, in_specs=placed, out_specs=P(("field", "tile"), None), check_vma=False
    )
```

```python
import functools

import jax
import jax.numpy as jnp
from jax import lax
from jax.experimental import pallas as pl
from jax.experimental.pallas import tpu as pltpu
from jax.sharding import PartitionSpec as P

XREACH = 64
RREACH = 8
LANES = 128
GROUP = 16
PARTS = 2
PIECES = 2
VMEM = pl.BlockSpec(memory_space=pltpu.VMEM)
SMEM = pl.BlockSpec(memory_space=pltpu.SMEM)
LIMIT = pltpu.CompilerParams(vmem_limit_bytes=32 * 1024 * 1024)


def pack_kernel(capacity, *refs):
    given, out_ref, (diag_ref, note_ref, used_ref, spot_ref), held, sems = (
        refs[:7], refs[7], refs[8:12], refs[12:19], refs[19]
    )
    copies = [
        pltpu.make_async_copy(source, target, sems.at[index])
        for index, (source, target) in enumerate(zip(given, held, strict=True))
    ]
    for copy in copies[::-1]:
        copy.start()
    tile_ref, cell_ref, id_ref, weight_ref, psi_ref, phi_ref, table_ref = held
    cells, epochs = psi_ref.shape[:2]
    tiles, width = used_ref.shape[0], psi_ref.shape[3]
    rows = psi_ref.shape[2]
    stride = 2 * capacity * rows + 1

    def clear(tile, carry):
        used_ref[tile] = 0
        note_ref[tile] = jnp.zeros(note_ref.shape[1:], jnp.float32)
        return carry

    lax.fori_loop(0, tiles, clear, 0, unroll=16)
    for copy in copies[:4]:
        copy.wait()

    lane = lax.broadcasted_iota(jnp.int32, (1, LANES), 1)
    for block in range(cells):
        for epoch in range(epochs):
            tile = tile_ref[block, 0, epoch]
            slot = used_ref[tile]
            used_ref[tile] = slot + 1
            spot_ref[block, epoch] = tile * stride + 2 * rows * slot
            place = (epoch * 2 * cells + cell_ref[block, epoch] + 1).astype(jnp.float32)
            note_ref[tile] = jnp.where(lane == slot, place, note_ref[tile])
    for copy in copies[4:]:
        copy.wait()

    source = lax.broadcasted_iota(jnp.int32, (width, width), 0)
    target = lax.broadcasted_iota(jnp.int32, (width, width), 1)
    for place in range(3):
        mask = source == target + (place - 1)
        for index in range(table_ref.shape[0]):
            row = jnp.sum(jnp.where(mask, table_ref[index], 0.0), axis=0, keepdims=True)
            diag_ref[index, place : place + 1, :] = row

    def write_note(tile, carry):
        out_ref[pl.ds(tile * stride + stride - 1, 1), :] = note_ref[tile]
        return carry

    lax.fori_loop(0, tiles, write_note, 0, unroll=16)
    for block in range(cells):
        for epoch in range(epochs):
            spot = spot_ref[block, epoch]
            bands = diag_ref[id_ref[block, epoch]] * weight_ref[block, epoch]
            for kind, ref in enumerate((psi_ref, phi_ref)):
                values = ref[block, epoch]
                out_ref[pl.ds(spot + kind * rows, rows), :] = (
                    values * bands[1:2]
                    + pltpu.roll(values, 1, 1) * bands[0:1]
                    + pltpu.roll(values, width - 1, 1) * bands[2:3]
                )


def sum_kernel(capacity, cells, in_ref, *refs):
    part_refs, sky_ref = refs[:-1], refs[-1]
    rows = sky_ref.shape[1]
    stride = 2 * capacity * rows + 1
    for index in range(sky_ref.shape[0]):
        sky_ref[index] = jnp.zeros(sky_ref.shape[1:], jnp.float32)

    def one_source(source, carry):
        first = source * stride
        notes = in_ref[pl.ds(first + stride - 1, 1), :].astype(jnp.int32)
        for slot in range(capacity):
            place = notes[0, slot] - 1
            there = place >= 0
            base = jnp.maximum(place, 0)
            for kind in range(2):
                value = in_ref[pl.ds(first + (2 * slot + kind) * rows, rows), :]
                value = jnp.where(there, value, 0.0)
                sky_ref[base + kind * cells] = sky_ref[base + kind * cells] + value
        return carry

    lax.fori_loop(0, in_ref.shape[0] // stride, one_source, 0, unroll=16)
    first = 0
    for ref in part_refs:
        for index in range(ref.shape[0]):
            ref[index] = sky_ref[(first + index) % sky_ref.shape[0]]
        first += ref.shape[0]


def windows_at(ref, epoch, start_row, start_col, rows):
    first = lax.shift_right_logical(start_col, 7)
    shift = start_col & (LANES - 1)
    turn = (LANES - shift) & (LANES - 1)
    mask = lax.broadcasted_iota(jnp.int32, (rows, LANES), 1) >= shift
    windows = []
    for kind in range(2):
        parts = [
            ref[epoch, kind, first + step, pl.ds(start_row, rows), :]
            for step in range(ref.shape[2] - 1)
        ]
        windows.append(
            [
                pltpu.roll(jnp.where(mask, parts[cell], parts[cell + 1]), turn, 1)
                for cell in range(len(parts) - 1)
            ]
        )
    return windows


def clear_sides(ref, epoch, kind):
    for side in (0, ref.shape[2] - 1):
        ref[epoch, kind, side] = jnp.zeros(ref.shape[3:], jnp.float32)


def tile_of(refs, index):
    for ref in refs:
        if index < ref.shape[0]:
            return ref[index]
        index -= ref.shape[0]


def near_kernel(tiles, group, split, pieces, row_ref, col_ref, me_ref, *refs):
    own_refs, twin_refs = refs[:PARTS], refs[PARTS : PARTS + pieces]
    sums_ref, *list_refs, count_ref, wide_ref = refs[PARTS + pieces :]
    epochs, vels = row_ref.shape
    cells, rows = sums_ref.shape[2:4]
    odd = me_ref[0] & 1
    towards = jnp.where((me_ref[0] == 0) | (me_ref[0] == tiles - 1), 0, 2 * odd - 1)
    twin_row = pl.multiple_of((1 - odd) * 2 * rows, rows)
    far_row = pl.multiple_of(odd * 2 * rows, rows)
    for epoch in range(epochs):
        for kind in range(2):
            clear_sides(wide_ref, epoch, kind)
            for cell in range(cells):
                index = (epoch * 2 + kind) * cells + cell
                at = wide_ref.at[epoch, kind, cell + 1]
                at[rows : 2 * rows, :] = tile_of(own_refs, index)
                at[pl.ds(twin_row, rows), :] = tile_of(twin_refs, index)
                at[pl.ds(far_row, rows), :] = jnp.zeros((rows, LANES), jnp.float32)

    def one_velocity(vel, counts):
        counts = list(counts)
        sums = [[jnp.zeros((rows, LANES), jnp.float32) for _ in range(cells)] for _ in range(2)]
        for epoch in range(epochs):
            row = row_ref[epoch, vel]
            start_col = LANES + col_ref[epoch, vel]
            windows = windows_at(wide_ref, epoch, rows + row, start_col, rows)
            for kind in range(2):
                for cell in range(cells):
                    sums[kind][cell] = sums[kind][cell] + windows[kind][cell]
            part = int(epoch >= split[0])
            place = epoch - part * split[0]
            start_row = row + (1 - odd) * rows
            code = (vel << 24) | (place << 16) | (start_row << 10) | start_col
            list_refs[part][counts[part]] = code
            counts[part] = counts[part] + jnp.where(row * towards > 0, 1, 0)
        for kind in range(2):
            for cell in range(cells):
                sums_ref[vel, kind, cell] = sums[kind][cell]
        return counts

    counts = lax.fori_loop(0, vels, one_velocity, [jnp.int32(0)] * PARTS, unroll=4)
    for part, count in enumerate(counts):
        for index in range(group):
            list_refs[part][count + index] = (((1 - odd) * rows) << 10) | LANES
        count_ref[part] = count
    count_ref[PARTS] = odd


def far_kernel(part, group, list_ref, count_ref, far_ref, given_ref, sums_ref, *refs):
    *best_refs, wide_ref = refs
    vels, _, cells, rows, _ = sums_ref.shape
    odd = count_ref[PARTS]
    far_row = pl.multiple_of(odd * rows, rows)
    zero_row = pl.multiple_of((1 - odd) * rows, rows)
    for epoch in range(wide_ref.shape[0]):
        for kind in range(2):
            clear_sides(wide_ref, epoch, kind)
            for cell in range(cells):
                at = wide_ref.at[epoch, kind, cell + 1]
                at[pl.ds(far_row, rows), :] = far_ref[(epoch * 2 + kind) * cells + cell]
                at[pl.ds(zero_row, rows), :] = jnp.zeros((rows, LANES), jnp.float32)

    def one_group(turn, carry):
        found = []
        for index in range(group):
            code = list_ref[turn * group + index]
            start_col = code & 1023
            start_row = (code >> 10) & 63
            epoch = (code >> 16) & 255
            found.append((code >> 24, windows_at(wide_ref, epoch, start_row, start_col, rows)))
        for vel, windows in found:
            for kind in range(2):
                for cell in range(cells):
                    sums_ref[vel, kind, cell] = sums_ref[vel, kind, cell] + windows[kind][cell]
        return carry

    lax.fori_loop(0, lax.div(count_ref[part] + group - 1, group), one_group, 0)
    for best_ref in best_refs:
        highest = [jnp.full((rows, LANES), -jnp.inf, jnp.float32) for _ in range(cells)]
        for vel in range(vels):
            for cell in range(cells):
                scale = lax.rsqrt(jnp.maximum(sums_ref[vel, 1, cell], 1.0))
                highest[cell] = jnp.maximum(highest[cell], sums_ref[vel, 0, cell] * scale)
        for cell in range(cells):
            best_ref[:, cell * LANES : (cell + 1) * LANES] = highest[cell]


def body(psi, phi, dest_tile, dest_cell, kernel_id, weight, kernels, row_offsets, col_offsets):
    tiles = lax.axis_size("tile")
    cells, epochs, rows, width = psi.shape
    capacity = max(2, 2 * cells * epochs // tiles)
    stride = 2 * capacity * rows + 1
    message = (tiles * stride, width)
    given = (jnp.swapaxes(dest_tile, 1, 2), dest_cell, kernel_id, weight, psi, phi, kernels)
    outgoing = pl.pallas_call(
        functools.partial(pack_kernel, capacity),
        out_shape=jax.ShapeDtypeStruct(message, jnp.float32),
        in_specs=[pl.BlockSpec(memory_space=pl.ANY)] * 7,
        out_specs=VMEM,
        scratch_shapes=[
            pltpu.VMEM((kernels.shape[0], 3, width), jnp.float32),
            pltpu.VMEM((tiles, 1, LANES), jnp.float32),
            pltpu.SMEM((tiles,), jnp.int32),
            pltpu.SMEM((cells, epochs), jnp.int32),
        ]
        + [pltpu.SMEM(array.shape, array.dtype) for array in given[:4]]
        + [pltpu.VMEM(array.shape, array.dtype) for array in given[4:]]
        + [pltpu.SemaphoreType.DMA((7,))],
        compiler_params=pltpu.CompilerParams(vmem_limit_bytes=32 * 1024 * 1024),
        name="pack",
    )(*(pltpu.with_memory_space_constraint(array, pltpu.HBM) for array in given))
    outgoing = outgoing.reshape(tiles, stride, 1, width)
    incoming = lax.all_to_all(outgoing, "tile", split_axis=0, concat_axis=0, tiled=True)
    incoming = incoming.reshape(message)
    total = epochs * 2 * cells
    split = [epochs - 3 * epochs // 8, 3 * epochs // 8]
    skies = pl.pallas_call(
        functools.partial(sum_kernel, capacity, cells),
        out_shape=[
            jax.ShapeDtypeStruct((count * 2 * cells, rows, width), jnp.float32)
            for count in split + [epochs // PIECES] * PIECES
        ],
        in_specs=[VMEM],
        out_specs=[VMEM] * (PARTS + PIECES),
        scratch_shapes=[pltpu.VMEM((total, rows, width), jnp.float32)],
        compiler_params=LIMIT,
        name="sum_slots",
    )(incoming)
    own, pieces = skies[:PARTS], skies[PARTS:]
    fields = lax.axis_size("field")
    pairs = [(f * tiles + i, f * tiles + i + 1) for f in range(fields) for i in range(1, tiles - 1, 2)]
    pairs += [
        (f * tiles + i, (f + 1) * tiles + i) for f in range(0, fields - 1, 2) for i in (0, tiles - 1)
    ]
    both = [way for a, b in pairs for way in ((a, b), (b, a))]
    far = [lax.ppermute(part, ("field", "tile"), both) for part in own]
    twin = [lax.ppermute(piece, "tile", [(i, i ^ 1) for i in range(tiles)]) for piece in pieces]
    me = lax.axis_index("tile").reshape(1)
    vels = row_offsets.shape[1]
    sums_shape = jax.ShapeDtypeStruct((vels, 2, cells, rows, width), jnp.float32)
    sums, *lists, count = pl.pallas_call(
        functools.partial(near_kernel, tiles, GROUP, split, PIECES),
        out_shape=[sums_shape]
        + [pltpu.SMEM((vels * count + GROUP,), jnp.int32) for count in split]
        + [pltpu.SMEM((PARTS + 1,), jnp.int32)],
        in_specs=[SMEM] * 3 + [VMEM] * (PARTS + PIECES),
        out_specs=[VMEM] + [SMEM] * (PARTS + 1),
        scratch_shapes=[pltpu.VMEM((epochs, 2, cells + 2, 3 * rows, width), jnp.float32)],
        compiler_params=LIMIT,
        name="stack_near",
    )(row_offsets, col_offsets, me, *own, *twin)
    for part in range(PARTS):
        last = part == PARTS - 1
        sums, *best = pl.pallas_call(
            functools.partial(far_kernel, part, GROUP),
            out_shape=[sums_shape]
            + [jax.ShapeDtypeStruct((rows, cells * width), jnp.float32)] * last,
            in_specs=[SMEM] * 2 + [VMEM] * 2,
            out_specs=[VMEM] * (1 + last),
            input_output_aliases={3: 0},
            scratch_shapes=[
                pltpu.VMEM((split[part], 2, cells + 2, 2 * rows, width), jnp.float32)
            ],
            compiler_params=LIMIT,
            name="stack_far",
        )(lists[part], count, far[part], sums)
    return best[0]


def solution(mesh):
    placed = (
        P(("field", "tile"), None, None, None),
        P(("field", "tile"), None, None, None),
        P(("field", "tile"), None, None),
        P(("field", "tile"), None),
        P(("field", "tile"), None),
        P(("field", "tile"), None),
        P(),
        P("field", None),
        P("field", None),
    )
    return jax.shard_map(
        body, mesh=mesh, in_specs=placed, out_specs=P(("field", "tile"), None), check_vma=False
    )
```

```python
import functools

import jax
import jax.numpy as jnp
from jax import lax
from jax.experimental import pallas as pl
from jax.experimental.pallas import tpu as pltpu
from jax.sharding import PartitionSpec as P

XREACH = 64
RREACH = 8
LANES = 128
GROUP = 16
PARTS = 2
ORDER = (4, 5, 2, 3, 7, 6, 1)
PIECES = 2
VMEM = pl.BlockSpec(memory_space=pltpu.VMEM)
SMEM = pl.BlockSpec(memory_space=pltpu.SMEM)
LIMIT = pltpu.CompilerParams(vmem_limit_bytes=32 * 1024 * 1024)


def pack_kernel(capacity, outputs, *refs):
    given, out_refs, rest = refs[:8], refs[8 : 8 + outputs], refs[8 + outputs :]
    (slots_ref, diag_ref, note_ref, used_ref, spot_ref), held, sems = rest[:5], rest[5:13], rest[13]
    copies = [
        pltpu.make_async_copy(source, target, sems.at[index])
        for index, (source, target) in enumerate(zip(given, held, strict=True))
    ]
    for copy in copies[::-1]:
        copy.start()
    tile_ref, cell_ref, id_ref, weight_ref, base_ref, psi_ref, phi_ref, table_ref = held
    cells, epochs, rows, width = psi_ref.shape
    chips = note_ref.shape[0]
    stride = 4 * capacity * rows + 1

    def clear(tile, carry):
        used_ref[tile] = 0
        return carry

    lax.fori_loop(0, used_ref.shape[0], clear, 0, unroll=16)
    note_ref[...] = jnp.zeros(note_ref.shape, jnp.float32)
    for copy in copies[:5]:
        copy.wait()

    lane = lax.broadcasted_iota(jnp.int32, (1, LANES), 1)
    for block in range(cells):
        for epoch in range(epochs):
            tile = tile_ref[block, 0, epoch] ^ base_ref[0]
            chip, core = tile >> 1, tile & 1
            slot = used_ref[tile]
            used_ref[tile] = slot + 1
            slot = core * capacity + slot
            spot_ref[block, epoch] = chip * stride + 2 * rows * slot
            place = (epoch * 2 * cells + cell_ref[block, epoch] + 1).astype(jnp.float32)
            note_ref[chip] = jnp.where(lane == slot, place, note_ref[chip])
    for copy in copies[5:]:
        copy.wait()

    source = lax.broadcasted_iota(jnp.int32, (width, width), 0)
    target = lax.broadcasted_iota(jnp.int32, (width, width), 1)
    for place in range(3):
        mask = source == target + (place - 1)
        for index in range(table_ref.shape[0]):
            row = jnp.sum(jnp.where(mask, table_ref[index], 0.0), axis=0, keepdims=True)
            diag_ref[index, place : place + 1, :] = row

    def write_note(chip, carry):
        slots_ref[pl.ds(chip * stride + stride - 1, 1), :] = note_ref[chip]
        return carry

    lax.fori_loop(0, chips, write_note, 0, unroll=8)
    for block in range(cells):
        for epoch in range(epochs):
            spot = spot_ref[block, epoch]
            bands = diag_ref[id_ref[block, epoch]] * weight_ref[block, epoch]
            for kind, ref in enumerate((psi_ref, phi_ref)):
                values = ref[block, epoch]
                slots_ref[pl.ds(spot + kind * rows, rows), :] = (
                    values * bands[1:2]
                    + pltpu.roll(values, 1, 1) * bands[0:1]
                    + pltpu.roll(values, width - 1, 1) * bands[2:3]
                )
    first = 0
    for out_ref in out_refs:
        count = out_ref.shape[0]
        flat_ref = out_ref.reshape(count, width)
        for row in range(0, count, rows):
            size = min(rows, count - row)
            flat_ref[row : row + size, :] = slots_ref[first + row : first + row + size, :]
        first += count


def sum_kernel(capacity, cells, *refs):
    in_refs, sky_refs = refs[:-2], refs[-2:]
    rows, width = sky_refs[0].shape[1:]
    stride = 4 * capacity * rows + 1
    for sky_ref in sky_refs:
        for index in range(sky_ref.shape[0]):
            sky_ref[index] = jnp.zeros((rows, width), jnp.float32)
    for in_ref in in_refs:
        flat_ref = in_ref.reshape(in_ref.shape[0], width)

        def one_message(message, carry, flat_ref=flat_ref):
            first = message * stride
            notes = flat_ref[pl.ds(first + stride - 1, 1), :].astype(jnp.int32)
            for slot in range(2 * capacity):
                sky_ref = sky_refs[slot // capacity]
                place = notes[0, slot] - 1
                there = place >= 0
                base = jnp.maximum(place, 0)
                for kind in range(2):
                    value = flat_ref[pl.ds(first + (2 * slot + kind) * rows, rows), :]
                    value = jnp.where(there, value, 0.0)
                    sky_ref[base + kind * cells] = sky_ref[base + kind * cells] + value
            return carry

        messages = in_ref.shape[0] // stride
        if messages == 1:
            one_message(0, 0)
        else:
            lax.fori_loop(0, messages, one_message, 0, unroll=8)


def join_kernel(mine_ref, other_ref, *part_refs):
    total = mine_ref.shape[0]
    first = 0
    for part_ref in part_refs:
        for index in range(part_ref.shape[0]):
            place = (first + index) % total
            part_ref[index] = mine_ref[place] + other_ref[place]
        first += part_ref.shape[0]


def windows_at(ref, epoch, start_row, start_col, rows):
    first = lax.shift_right_logical(start_col, 7)
    shift = start_col & (LANES - 1)
    turn = (LANES - shift) & (LANES - 1)
    mask = lax.broadcasted_iota(jnp.int32, (rows, LANES), 1) >= shift
    windows = []
    for kind in range(2):
        parts = [
            ref[epoch, kind, first + step, pl.ds(start_row, rows), :]
            for step in range(ref.shape[2] - 1)
        ]
        windows.append(
            [
                pltpu.roll(jnp.where(mask, parts[cell], parts[cell + 1]), turn, 1)
                for cell in range(len(parts) - 1)
            ]
        )
    return windows


def clear_sides(ref, epoch, kind):
    for side in (0, ref.shape[2] - 1):
        ref[epoch, kind, side] = jnp.zeros(ref.shape[3:], jnp.float32)


def tile_of(refs, index):
    for ref in refs:
        if index < ref.shape[0]:
            return ref[index]
        index -= ref.shape[0]


def near_kernel(tiles, group, split, pieces, row_ref, col_ref, me_ref, *refs):
    own_refs, twin_refs = refs[:PARTS], refs[PARTS : PARTS + pieces]
    sums_ref, *list_refs, count_ref, wide_ref = refs[PARTS + pieces :]
    epochs, vels = row_ref.shape
    cells, rows = sums_ref.shape[2:4]
    odd = me_ref[0] & 1
    towards = jnp.where((me_ref[0] == 0) | (me_ref[0] == tiles - 1), 0, 2 * odd - 1)
    twin_row = pl.multiple_of((1 - odd) * 2 * rows, rows)
    far_row = pl.multiple_of(odd * 2 * rows, rows)
    for epoch in range(epochs):
        for kind in range(2):
            clear_sides(wide_ref, epoch, kind)
            for cell in range(cells):
                index = (epoch * 2 + kind) * cells + cell
                at = wide_ref.at[epoch, kind, cell + 1]
                at[rows : 2 * rows, :] = tile_of(own_refs, index)
                at[pl.ds(twin_row, rows), :] = tile_of(twin_refs, index)
                at[pl.ds(far_row, rows), :] = jnp.zeros((rows, LANES), jnp.float32)

    def one_velocity(vel, counts):
        counts = list(counts)
        sums = [[jnp.zeros((rows, LANES), jnp.float32) for _ in range(cells)] for _ in range(2)]
        for epoch in range(epochs):
            row = row_ref[epoch, vel]
            start_col = LANES + col_ref[epoch, vel]
            windows = windows_at(wide_ref, epoch, rows + row, start_col, rows)
            for kind in range(2):
                for cell in range(cells):
                    sums[kind][cell] = sums[kind][cell] + windows[kind][cell]
            part = int(epoch >= split[0])
            place = epoch - part * split[0]
            start_row = row + (1 - odd) * rows
            code = (vel << 24) | (place << 16) | (start_row << 10) | start_col
            list_refs[part][counts[part]] = code
            counts[part] = counts[part] + jnp.where(row * towards > 0, 1, 0)
        for kind in range(2):
            for cell in range(cells):
                sums_ref[vel, kind, cell] = sums[kind][cell]
        return counts

    counts = lax.fori_loop(0, vels, one_velocity, [jnp.int32(0)] * PARTS, unroll=4)
    for part, count in enumerate(counts):
        for index in range(group):
            list_refs[part][count + index] = (((1 - odd) * rows) << 10) | LANES
        count_ref[part] = count
    count_ref[PARTS] = odd


def far_kernel(part, group, list_ref, count_ref, far_ref, given_ref, sums_ref, *refs):
    *best_refs, wide_ref = refs
    vels, _, cells, rows, _ = sums_ref.shape
    odd = count_ref[PARTS]
    far_row = pl.multiple_of(odd * rows, rows)
    zero_row = pl.multiple_of((1 - odd) * rows, rows)
    for epoch in range(wide_ref.shape[0]):
        for kind in range(2):
            clear_sides(wide_ref, epoch, kind)
            for cell in range(cells):
                at = wide_ref.at[epoch, kind, cell + 1]
                at[pl.ds(far_row, rows), :] = far_ref[(epoch * 2 + kind) * cells + cell]
                at[pl.ds(zero_row, rows), :] = jnp.zeros((rows, LANES), jnp.float32)

    def one_group(turn, carry):
        found = []
        for index in range(group):
            code = list_ref[turn * group + index]
            start_col = code & 1023
            start_row = (code >> 10) & 63
            epoch = (code >> 16) & 255
            found.append((code >> 24, windows_at(wide_ref, epoch, start_row, start_col, rows)))
        for vel, windows in found:
            for kind in range(2):
                for cell in range(cells):
                    sums_ref[vel, kind, cell] = sums_ref[vel, kind, cell] + windows[kind][cell]
        return carry

    lax.fori_loop(0, lax.div(count_ref[part] + group - 1, group), one_group, 0)
    for best_ref in best_refs:
        highest = [jnp.full((rows, LANES), -jnp.inf, jnp.float32) for _ in range(cells)]
        for vel in range(vels):
            for cell in range(cells):
                scale = lax.rsqrt(jnp.maximum(sums_ref[vel, 1, cell], 1.0))
                highest[cell] = jnp.maximum(highest[cell], sums_ref[vel, 0, cell] * scale)
        for cell in range(cells):
            best_ref[:, cell * LANES : (cell + 1) * LANES] = highest[cell]


def body(psi, phi, dest_tile, dest_cell, kernel_id, weight, kernels, row_offsets, col_offsets):
    tiles = lax.axis_size("tile")
    cells, epochs, rows, width = psi.shape
    capacity = max(2, 2 * cells * epochs // tiles)
    chips = tiles // 2
    stride = 4 * capacity * rows + 1
    me = lax.axis_index("tile")
    direct = chips <= len(ORDER) + 1
    base = me if direct else me & 1
    given = (jnp.swapaxes(dest_tile, 1, 2), dest_cell, kernel_id, weight, base.reshape(1))
    given += (psi, phi, kernels)
    outputs = chips if direct else 1
    outgoing = pl.pallas_call(
        functools.partial(pack_kernel, capacity, outputs),
        out_shape=[
            jax.ShapeDtypeStruct((chips * stride // outputs, 1, width), jnp.float32)
            for _ in range(outputs)
        ],
        in_specs=[pl.BlockSpec(memory_space=pl.ANY)] * len(given),
        out_specs=[VMEM] * outputs,
        scratch_shapes=[
            pltpu.VMEM((chips * stride, width), jnp.float32),
            pltpu.VMEM((kernels.shape[0], 3, width), jnp.float32),
            pltpu.VMEM((chips, 1, LANES), jnp.float32),
            pltpu.SMEM((tiles,), jnp.int32),
            pltpu.SMEM((cells, epochs), jnp.int32),
        ]
        + [pltpu.SMEM(array.shape, array.dtype) for array in given[:5]]
        + [pltpu.VMEM(array.shape, array.dtype) for array in given[5:]]
        + [pltpu.SemaphoreType.DMA((len(given),))],
        compiler_params=LIMIT,
        name="pack",
    )(*(pltpu.with_memory_space_constraint(array, pltpu.HBM) for array in given))
    if direct:
        incoming = [outgoing[0]] + [
            lax.ppermute(outgoing[k], "tile", [(i, i ^ (2 * k)) for i in range(tiles)])
            for k in ORDER
            if k < chips
        ]
    else:
        incoming = lax.all_to_all(
            outgoing[0].reshape(chips, stride, 1, width),
            "tile",
            split_axis=0,
            concat_axis=0,
            axis_index_groups=[list(range(core, tiles, 2)) for core in range(2)],
            tiled=True,
        )
        incoming = [incoming.reshape(chips * stride, 1, width)]
    total = epochs * 2 * cells
    sky_shape = jax.ShapeDtypeStruct((total, rows, width), jnp.float32)
    mine, others = pl.pallas_call(
        functools.partial(sum_kernel, capacity, cells),
        out_shape=[sky_shape, sky_shape],
        in_specs=[VMEM] * len(incoming),
        out_specs=[VMEM, VMEM],
        compiler_params=LIMIT,
        name="sum_slots",
    )(*incoming)
    other = lax.ppermute(others, "tile", [(i, i ^ 1) for i in range(tiles)])
    split = [epochs - 3 * epochs // 8, 3 * epochs // 8]
    skies = pl.pallas_call(
        join_kernel,
        out_shape=[
            jax.ShapeDtypeStruct((count * 2 * cells, rows, width), jnp.float32)
            for count in split + [epochs // PIECES] * PIECES
        ],
        in_specs=[VMEM, VMEM],
        out_specs=[VMEM] * (PARTS + PIECES),
        compiler_params=LIMIT,
        name="join",
    )(mine, other)
    own, pieces = skies[:PARTS], skies[PARTS:]
    fields = lax.axis_size("field")
    pairs = [(f * tiles + i, f * tiles + i + 1) for f in range(fields) for i in range(1, tiles - 1, 2)]
    pairs += [
        (f * tiles + i, (f + 1) * tiles + i) for f in range(0, fields - 1, 2) for i in (0, tiles - 1)
    ]
    both = [way for a, b in pairs for way in ((a, b), (b, a))]
    far = [lax.ppermute(part, ("field", "tile"), both) for part in own]
    twin = [lax.ppermute(piece, "tile", [(i, i ^ 1) for i in range(tiles)]) for piece in pieces]
    vels = row_offsets.shape[1]
    sums_shape = jax.ShapeDtypeStruct((vels, 2, cells, rows, width), jnp.float32)
    sums, *lists, count = pl.pallas_call(
        functools.partial(near_kernel, tiles, GROUP, split, PIECES),
        out_shape=[sums_shape]
        + [pltpu.SMEM((vels * count + GROUP,), jnp.int32) for count in split]
        + [pltpu.SMEM((PARTS + 1,), jnp.int32)],
        in_specs=[SMEM] * 3 + [VMEM] * (PARTS + PIECES),
        out_specs=[VMEM] + [SMEM] * (PARTS + 1),
        scratch_shapes=[pltpu.VMEM((epochs, 2, cells + 2, 3 * rows, width), jnp.float32)],
        compiler_params=LIMIT,
        name="stack_near",
    )(row_offsets, col_offsets, me.reshape(1), *own, *twin)
    for part in range(PARTS):
        last = part == PARTS - 1
        sums, *best = pl.pallas_call(
            functools.partial(far_kernel, part, GROUP),
            out_shape=[sums_shape]
            + [jax.ShapeDtypeStruct((rows, cells * width), jnp.float32)] * last,
            in_specs=[SMEM] * 2 + [VMEM] * 2,
            out_specs=[VMEM] * (1 + last),
            input_output_aliases={3: 0},
            scratch_shapes=[
                pltpu.VMEM((split[part], 2, cells + 2, 2 * rows, width), jnp.float32)
            ],
            compiler_params=LIMIT,
            name="stack_far",
        )(lists[part], count, far[part], sums)
    return best[0]


def solution(mesh):
    placed = (
        P(("field", "tile"), None, None, None),
        P(("field", "tile"), None, None, None),
        P(("field", "tile"), None, None),
        P(("field", "tile"), None),
        P(("field", "tile"), None),
        P(("field", "tile"), None),
        P(),
        P("field", None),
        P("field", None),
    )
    return jax.shard_map(
        body, mesh=mesh, in_specs=placed, out_specs=P(("field", "tile"), None), check_vma=False
    )
```

```python
import functools

import jax
import jax.numpy as jnp
from jax import lax
from jax.experimental import pallas as pl
from jax.experimental.pallas import tpu as pltpu
from jax.sharding import PartitionSpec as P

XREACH = 64
RREACH = 8
LANES = 128
GROUP = 16
PARTS = 2
EARLY = 6
ORDER = (4, 2, 5, 3, 7, 6, 1)
VMEM = pl.BlockSpec(memory_space=pltpu.VMEM)
SMEM = pl.BlockSpec(memory_space=pltpu.SMEM)
LIMIT = pltpu.CompilerParams(vmem_limit_bytes=32 * 1024 * 1024)


def pack_kernel(capacity, outputs, *refs):
    given, out_refs, rest = refs[:8], refs[8 : 8 + outputs], refs[8 + outputs :]
    (slots_ref, diag_ref, note_ref, used_ref, spot_ref), held, sems = rest[:5], rest[5:13], rest[13]
    copies = [
        pltpu.make_async_copy(source, target, sems.at[index])
        for index, (source, target) in enumerate(zip(given, held, strict=True))
    ]
    for copy in copies[::-1]:
        copy.start()
    tile_ref, cell_ref, id_ref, weight_ref, base_ref, psi_ref, phi_ref, table_ref = held
    cells, epochs, rows, width = psi_ref.shape
    chips = note_ref.shape[0]
    stride = 4 * capacity * rows + 1

    def clear(tile, carry):
        used_ref[tile] = 0
        return carry

    lax.fori_loop(0, used_ref.shape[0], clear, 0, unroll=16)
    note_ref[...] = jnp.zeros(note_ref.shape, jnp.float32)
    for copy in copies[:5]:
        copy.wait()

    lane = lax.broadcasted_iota(jnp.int32, (1, LANES), 1)
    for block in range(cells):
        for epoch in range(epochs):
            tile = tile_ref[block, 0, epoch] ^ base_ref[0]
            chip, core = tile >> 1, tile & 1
            slot = used_ref[tile]
            used_ref[tile] = slot + 1
            slot = core * capacity + slot
            spot_ref[block, epoch] = chip * stride + 2 * rows * slot
            place = (epoch * 2 * cells + cell_ref[block, epoch] + 1).astype(jnp.float32)
            note_ref[chip] = jnp.where(lane == slot, place, note_ref[chip])
    for copy in copies[5:]:
        copy.wait()

    source = lax.broadcasted_iota(jnp.int32, (width, width), 0)
    target = lax.broadcasted_iota(jnp.int32, (width, width), 1)
    for place in range(3):
        mask = source == target + (place - 1)
        for index in range(table_ref.shape[0]):
            row = jnp.sum(jnp.where(mask, table_ref[index], 0.0), axis=0, keepdims=True)
            diag_ref[index, place : place + 1, :] = row

    def write_note(chip, carry):
        slots_ref[pl.ds(chip * stride + stride - 1, 1), :] = note_ref[chip]
        return carry

    lax.fori_loop(0, chips, write_note, 0, unroll=8)
    for block in range(cells):
        for epoch in range(epochs):
            spot = spot_ref[block, epoch]
            bands = diag_ref[id_ref[block, epoch]] * weight_ref[block, epoch]
            for kind, ref in enumerate((psi_ref, phi_ref)):
                values = ref[block, epoch]
                slots_ref[pl.ds(spot + kind * rows, rows), :] = (
                    values * bands[1:2]
                    + pltpu.roll(values, 1, 1) * bands[0:1]
                    + pltpu.roll(values, width - 1, 1) * bands[2:3]
                )
    first = 0
    for out_ref in out_refs:
        count = out_ref.shape[0]
        flat_ref = out_ref.reshape(count, width)
        for row in range(0, count, rows):
            size = min(rows, count - row)
            flat_ref[row : row + size, :] = slots_ref[first + row : first + row + size, :]
        first += count


def sum_kernel(capacity, cells, first_call, *refs):
    in_refs, sky_refs = refs[: -2 if first_call else -4], refs[-2:]
    rows, width = sky_refs[0].shape[1:]
    stride = 4 * capacity * rows + 1
    for sky_ref in sky_refs if first_call else ():
        for index in range(sky_ref.shape[0]):
            sky_ref[index] = jnp.zeros((rows, width), jnp.float32)
    for in_ref in in_refs:
        flat_ref = in_ref.reshape(in_ref.shape[0], width)

        def one_message(message, carry, flat_ref=flat_ref):
            first = message * stride
            notes = flat_ref[pl.ds(first + stride - 1, 1), :].astype(jnp.int32)
            for slot in range(2 * capacity):
                sky_ref = sky_refs[slot // capacity]
                place = notes[0, slot] - 1
                there = place >= 0
                base = jnp.maximum(place, 0)
                for kind in range(2):
                    value = flat_ref[pl.ds(first + (2 * slot + kind) * rows, rows), :]
                    value = jnp.where(there, value, 0.0)
                    sky_ref[base + kind * cells] = sky_ref[base + kind * cells] + value
            return carry

        messages = in_ref.shape[0] // stride
        if messages == 1:
            one_message(0, 0)
        else:
            lax.fori_loop(0, messages, one_message, 0, unroll=8)


def join_kernel(mine_ref, other_ref, *part_refs):
    first = 0
    for part_ref in part_refs:
        for index in range(part_ref.shape[0]):
            part_ref[index] = mine_ref[first + index] + other_ref[first + index]
        first += part_ref.shape[0]


def windows_at(ref, epoch, start_row, start_col, rows):
    first = lax.shift_right_logical(start_col, 7)
    shift = start_col & (LANES - 1)
    turn = (LANES - shift) & (LANES - 1)
    mask = lax.broadcasted_iota(jnp.int32, (rows, LANES), 1) >= shift
    windows = []
    for kind in range(2):
        parts = [
            ref[epoch, kind, first + step, pl.ds(start_row, rows), :]
            for step in range(ref.shape[2] - 1)
        ]
        windows.append(
            [
                pltpu.roll(jnp.where(mask, parts[cell], parts[cell + 1]), turn, 1)
                for cell in range(len(parts) - 1)
            ]
        )
    return windows


def clear_sides(ref, epoch, kind):
    for side in (0, ref.shape[2] - 1):
        ref[epoch, kind, side] = jnp.zeros(ref.shape[3:], jnp.float32)


def tile_of(refs, index):
    for ref in refs:
        if index < ref.shape[0]:
            return ref[index]
        index -= ref.shape[0]


def near_kernel(tiles, group, split, row_ref, col_ref, me_ref, *refs):
    own_refs, twin_refs = refs[:PARTS], refs[PARTS : PARTS + 2]
    sums_ref, *list_refs, count_ref, wide_ref = refs[PARTS + 2 :]
    epochs, vels = row_ref.shape
    cells, rows = sums_ref.shape[2:4]
    odd = me_ref[0] & 1
    towards = jnp.where((me_ref[0] == 0) | (me_ref[0] == tiles - 1), 0, 2 * odd - 1)
    twin_row = pl.multiple_of((1 - odd) * 2 * rows, rows)
    far_row = pl.multiple_of(odd * 2 * rows, rows)
    for epoch in range(epochs):
        for kind in range(2):
            clear_sides(wide_ref, epoch, kind)
            for cell in range(cells):
                index = (epoch * 2 + kind) * cells + cell
                at = wide_ref.at[epoch, kind, cell + 1]
                at[rows : 2 * rows, :] = tile_of(own_refs, index)
                at[pl.ds(twin_row, rows), :] = twin_refs[0][index] + twin_refs[1][index]
                at[pl.ds(far_row, rows), :] = jnp.zeros((rows, LANES), jnp.float32)

    def one_velocity(vel, counts):
        counts = list(counts)
        sums = [[jnp.zeros((rows, LANES), jnp.float32) for _ in range(cells)] for _ in range(2)]
        for epoch in range(epochs):
            row = row_ref[epoch, vel]
            start_col = LANES + col_ref[epoch, vel]
            windows = windows_at(wide_ref, epoch, rows + row, start_col, rows)
            for kind in range(2):
                for cell in range(cells):
                    sums[kind][cell] = sums[kind][cell] + windows[kind][cell]
            part = int(epoch >= split[0])
            place = epoch - part * split[0]
            start_row = row + (1 - odd) * rows
            code = (vel << 24) | (place << 16) | (start_row << 10) | start_col
            list_refs[part][counts[part]] = code
            counts[part] = counts[part] + jnp.where(row * towards > 0, 1, 0)
        for kind in range(2):
            for cell in range(cells):
                sums_ref[vel, kind, cell] = sums[kind][cell]
        return counts

    counts = lax.fori_loop(0, vels, one_velocity, [jnp.int32(0)] * PARTS, unroll=4)
    for part, count in enumerate(counts):
        for index in range(group):
            list_refs[part][count + index] = (((1 - odd) * rows) << 10) | LANES
        count_ref[part] = count
    count_ref[PARTS] = odd


def far_kernel(part, group, list_ref, count_ref, far_ref, given_ref, sums_ref, *refs):
    *best_refs, wide_ref = refs
    vels, _, cells, rows, _ = sums_ref.shape
    odd = count_ref[PARTS]
    far_row = pl.multiple_of(odd * rows, rows)
    zero_row = pl.multiple_of((1 - odd) * rows, rows)
    for epoch in range(wide_ref.shape[0]):
        for kind in range(2):
            clear_sides(wide_ref, epoch, kind)
            for cell in range(cells):
                at = wide_ref.at[epoch, kind, cell + 1]
                at[pl.ds(far_row, rows), :] = far_ref[(epoch * 2 + kind) * cells + cell]
                at[pl.ds(zero_row, rows), :] = jnp.zeros((rows, LANES), jnp.float32)

    def one_group(turn, carry):
        found = []
        for index in range(group):
            code = list_ref[turn * group + index]
            start_col = code & 1023
            start_row = (code >> 10) & 63
            epoch = (code >> 16) & 255
            found.append((code >> 24, windows_at(wide_ref, epoch, start_row, start_col, rows)))
        for vel, windows in found:
            for kind in range(2):
                for cell in range(cells):
                    sums_ref[vel, kind, cell] = sums_ref[vel, kind, cell] + windows[kind][cell]
        return carry

    lax.fori_loop(0, lax.div(count_ref[part] + group - 1, group), one_group, 0)
    for best_ref in best_refs:
        highest = [jnp.full((rows, LANES), -jnp.inf, jnp.float32) for _ in range(cells)]
        for vel in range(vels):
            for cell in range(cells):
                scale = lax.rsqrt(jnp.maximum(sums_ref[vel, 1, cell], 1.0))
                highest[cell] = jnp.maximum(highest[cell], sums_ref[vel, 0, cell] * scale)
        for cell in range(cells):
            best_ref[:, cell * LANES : (cell + 1) * LANES] = highest[cell]


def body(psi, phi, dest_tile, dest_cell, kernel_id, weight, kernels, row_offsets, col_offsets):
    tiles = lax.axis_size("tile")
    cells, epochs, rows, width = psi.shape
    capacity = max(2, 2 * cells * epochs // tiles)
    chips = tiles // 2
    stride = 4 * capacity * rows + 1
    me = lax.axis_index("tile")
    direct = chips <= len(ORDER) + 1
    base = me if direct else me & 1
    given = (jnp.swapaxes(dest_tile, 1, 2), dest_cell, kernel_id, weight, base.reshape(1))
    given += (psi, phi, kernels)
    outputs = chips if direct else 1
    outgoing = pl.pallas_call(
        functools.partial(pack_kernel, capacity, outputs),
        out_shape=[
            jax.ShapeDtypeStruct((chips * stride // outputs, 1, width), jnp.float32)
            for _ in range(outputs)
        ],
        in_specs=[pl.BlockSpec(memory_space=pl.ANY)] * len(given),
        out_specs=[VMEM] * outputs,
        scratch_shapes=[
            pltpu.VMEM((chips * stride, width), jnp.float32),
            pltpu.VMEM((kernels.shape[0], 3, width), jnp.float32),
            pltpu.VMEM((chips, 1, LANES), jnp.float32),
            pltpu.SMEM((tiles,), jnp.int32),
            pltpu.SMEM((cells, epochs), jnp.int32),
        ]
        + [pltpu.SMEM(array.shape, array.dtype) for array in given[:5]]
        + [pltpu.VMEM(array.shape, array.dtype) for array in given[5:]]
        + [pltpu.SemaphoreType.DMA((len(given),))],
        compiler_params=LIMIT,
        name="pack",
    )(*(pltpu.with_memory_space_constraint(array, pltpu.HBM) for array in given))
    if direct:
        incoming = [outgoing[0]] + [
            lax.ppermute(outgoing[k], "tile", [(i, i ^ (2 * k)) for i in range(tiles)])
            for k in ORDER
            if k < chips
        ]
    else:
        incoming = lax.all_to_all(
            outgoing[0].reshape(chips, stride, 1, width),
            "tile",
            split_axis=0,
            concat_axis=0,
            axis_index_groups=[list(range(core, tiles, 2)) for core in range(2)],
            tiled=True,
        )
        incoming = [incoming.reshape(chips * stride, 1, width)]
    total = epochs * 2 * cells
    sky_shape = jax.ShapeDtypeStruct((total, rows, width), jnp.float32)
    skies = []
    for some in (incoming[:EARLY], incoming[EARLY:]):
        if some:
            skies = pl.pallas_call(
                functools.partial(sum_kernel, capacity, cells, not skies),
                out_shape=[sky_shape, sky_shape],
                in_specs=[VMEM] * (len(some) + len(skies)),
                out_specs=[VMEM, VMEM],
                input_output_aliases={len(some) + i: i for i in range(len(skies))},
                compiler_params=LIMIT,
                name="sum_slots",
            )(*some, *skies)
    mine, others = skies
    across = [(i, i ^ 1) for i in range(tiles)]
    other = lax.ppermute(others, "tile", across)
    theirs = lax.ppermute(mine, "tile", across)
    split = [epochs - 3 * epochs // 8, 3 * epochs // 8]
    own = pl.pallas_call(
        join_kernel,
        out_shape=[
            jax.ShapeDtypeStruct((count * 2 * cells, rows, width), jnp.float32)
            for count in split
        ],
        in_specs=[VMEM, VMEM],
        out_specs=[VMEM] * PARTS,
        compiler_params=LIMIT,
        name="join",
    )(mine, other)
    fields = lax.axis_size("field")
    pairs = [(f * tiles + i, f * tiles + i + 1) for f in range(fields) for i in range(1, tiles - 1, 2)]
    pairs += [
        (f * tiles + i, (f + 1) * tiles + i) for f in range(0, fields - 1, 2) for i in (0, tiles - 1)
    ]
    both = [way for a, b in pairs for way in ((a, b), (b, a))]
    far = [lax.ppermute(part, ("field", "tile"), both) for part in own]
    vels = row_offsets.shape[1]
    sums_shape = jax.ShapeDtypeStruct((vels, 2, cells, rows, width), jnp.float32)
    sums, *lists, count = pl.pallas_call(
        functools.partial(near_kernel, tiles, GROUP, split),
        out_shape=[sums_shape]
        + [pltpu.SMEM((vels * count + GROUP,), jnp.int32) for count in split]
        + [pltpu.SMEM((PARTS + 1,), jnp.int32)],
        in_specs=[SMEM] * 3 + [VMEM] * (PARTS + 2),
        out_specs=[VMEM] + [SMEM] * (PARTS + 1),
        scratch_shapes=[pltpu.VMEM((epochs, 2, cells + 2, 3 * rows, width), jnp.float32)],
        compiler_params=LIMIT,
        name="stack_near",
    )(row_offsets, col_offsets, me.reshape(1), *own, others, theirs)
    for part in range(PARTS):
        last = part == PARTS - 1
        sums, *best = pl.pallas_call(
            functools.partial(far_kernel, part, GROUP),
            out_shape=[sums_shape]
            + [jax.ShapeDtypeStruct((rows, cells * width), jnp.float32)] * last,
            in_specs=[SMEM] * 2 + [VMEM] * 2,
            out_specs=[VMEM] * (1 + last),
            input_output_aliases={3: 0},
            scratch_shapes=[
                pltpu.VMEM((split[part], 2, cells + 2, 2 * rows, width), jnp.float32)
            ],
            compiler_params=LIMIT,
            name="stack_far",
        )(lists[part], count, far[part], sums)
    return best[0]


def solution(mesh):
    placed = (
        P(("field", "tile"), None, None, None),
        P(("field", "tile"), None, None, None),
        P(("field", "tile"), None, None),
        P(("field", "tile"), None),
        P(("field", "tile"), None),
        P(("field", "tile"), None),
        P(),
        P("field", None),
        P("field", None),
    )
    return jax.shard_map(
        body, mesh=mesh, in_specs=placed, out_specs=P(("field", "tile"), None), check_vma=False
    )
```

```python
import functools

import jax
import jax.numpy as jnp
from jax import lax
from jax.experimental import pallas as pl
from jax.experimental.pallas import tpu as pltpu
from jax.sharding import PartitionSpec as P

XREACH = 64
RREACH = 8
LANES = 128
GROUP = 16
PARTS = 3
EARLY = 6
ORDER = (4, 2, 5, 3, 7, 6, 1)
VMEM = pl.BlockSpec(memory_space=pltpu.VMEM)
SMEM = pl.BlockSpec(memory_space=pltpu.SMEM)
LIMIT = pltpu.CompilerParams(vmem_limit_bytes=32 * 1024 * 1024)


def pack_kernel(capacity, outputs, *refs):
    given, out_refs, rest = refs[:8], refs[8 : 8 + outputs], refs[8 + outputs :]
    (slots_ref, diag_ref, note_ref, used_ref, spot_ref), held, sems = rest[:5], rest[5:13], rest[13]
    copies = [
        pltpu.make_async_copy(source, target, sems.at[index])
        for index, (source, target) in enumerate(zip(given, held, strict=True))
    ]
    for copy in copies[::-1]:
        copy.start()
    tile_ref, cell_ref, id_ref, weight_ref, base_ref, psi_ref, phi_ref, table_ref = held
    cells, epochs, rows, width = psi_ref.shape
    chips = note_ref.shape[0]
    stride = 4 * capacity * rows + 1

    def clear(tile, carry):
        used_ref[tile] = 0
        return carry

    lax.fori_loop(0, used_ref.shape[0], clear, 0, unroll=16)
    note_ref[...] = jnp.zeros(note_ref.shape, jnp.float32)
    for copy in copies[:5]:
        copy.wait()

    lane = lax.broadcasted_iota(jnp.int32, (1, LANES), 1)
    for block in range(cells):
        for epoch in range(epochs):
            tile = tile_ref[block, 0, epoch] ^ base_ref[0]
            chip, core = tile >> 1, tile & 1
            slot = used_ref[tile]
            used_ref[tile] = slot + 1
            slot = core * capacity + slot
            spot_ref[block, epoch] = chip * stride + 2 * rows * slot
            place = (epoch * 2 * cells + cell_ref[block, epoch] + 1).astype(jnp.float32)
            note_ref[chip] = jnp.where(lane == slot, place, note_ref[chip])
    for copy in copies[5:]:
        copy.wait()

    source = lax.broadcasted_iota(jnp.int32, (width, width), 0)
    target = lax.broadcasted_iota(jnp.int32, (width, width), 1)
    for place in range(3):
        mask = source == target + (place - 1)
        for index in range(table_ref.shape[0]):
            row = jnp.sum(jnp.where(mask, table_ref[index], 0.0), axis=0, keepdims=True)
            diag_ref[index, place : place + 1, :] = row

    def write_note(chip, carry):
        slots_ref[pl.ds(chip * stride + stride - 1, 1), :] = note_ref[chip]
        return carry

    lax.fori_loop(0, chips, write_note, 0, unroll=8)
    for block in range(cells):
        for epoch in range(epochs):
            spot = spot_ref[block, epoch]
            bands = diag_ref[id_ref[block, epoch]] * weight_ref[block, epoch]
            for kind, ref in enumerate((psi_ref, phi_ref)):
                values = ref[block, epoch]
                slots_ref[pl.ds(spot + kind * rows, rows), :] = (
                    values * bands[1:2]
                    + pltpu.roll(values, 1, 1) * bands[0:1]
                    + pltpu.roll(values, width - 1, 1) * bands[2:3]
                )
    first = 0
    for out_ref in out_refs:
        count = out_ref.shape[0]
        flat_ref = out_ref.reshape(count, width)
        for row in range(0, count, rows):
            size = min(rows, count - row)
            flat_ref[row : row + size, :] = slots_ref[first + row : first + row + size, :]
        first += count


def sum_kernel(capacity, cells, first_call, *refs):
    in_refs, sky_refs = refs[: -2 if first_call else -4], refs[-2:]
    rows, width = sky_refs[0].shape[1:]
    stride = 4 * capacity * rows + 1
    for sky_ref in sky_refs if first_call else ():
        for index in range(sky_ref.shape[0]):
            sky_ref[index] = jnp.zeros((rows, width), jnp.float32)
    for in_ref in in_refs:
        flat_ref = in_ref.reshape(in_ref.shape[0], width)

        def one_message(message, carry, flat_ref=flat_ref):
            first = message * stride
            notes = flat_ref[pl.ds(first + stride - 1, 1), :].astype(jnp.int32)
            for slot in range(2 * capacity):
                sky_ref = sky_refs[slot // capacity]
                place = notes[0, slot] - 1
                there = place >= 0
                base = jnp.maximum(place, 0)
                for kind in range(2):
                    value = flat_ref[pl.ds(first + (2 * slot + kind) * rows, rows), :]
                    value = jnp.where(there, value, 0.0)
                    sky_ref[base + kind * cells] = sky_ref[base + kind * cells] + value
            return carry

        messages = in_ref.shape[0] // stride
        if messages == 1:
            one_message(0, 0)
        else:
            lax.fori_loop(0, messages, one_message, 0, unroll=8)


def join_kernel(mine_ref, other_ref, *part_refs):
    first = 0
    for part_ref in part_refs:
        for index in range(part_ref.shape[0]):
            part_ref[index] = mine_ref[first + index] + other_ref[first + index]
        first += part_ref.shape[0]


def windows_at(ref, epoch, start_row, start_col, rows):
    first = lax.shift_right_logical(start_col, 7)
    shift = start_col & (LANES - 1)
    turn = (LANES - shift) & (LANES - 1)
    mask = lax.broadcasted_iota(jnp.int32, (rows, LANES), 1) >= shift
    windows = []
    for kind in range(2):
        parts = [
            ref[epoch, kind, first + step, pl.ds(start_row, rows), :]
            for step in range(ref.shape[2] - 1)
        ]
        windows.append(
            [
                pltpu.roll(jnp.where(mask, parts[cell], parts[cell + 1]), turn, 1)
                for cell in range(len(parts) - 1)
            ]
        )
    return windows


def clear_sides(ref, epoch, kind):
    for side in (0, ref.shape[2] - 1):
        ref[epoch, kind, side] = jnp.zeros(ref.shape[3:], jnp.float32)


def tile_of(refs, index):
    for ref in refs:
        if index < ref.shape[0]:
            return ref[index]
        index -= ref.shape[0]


def near_kernel(tiles, group, split, row_ref, col_ref, me_ref, *refs):
    own_refs, twin_refs = refs[:PARTS], refs[PARTS : PARTS + 2]
    sums_ref, *list_refs, count_ref, wide_ref = refs[PARTS + 2 :]
    epochs, vels = row_ref.shape
    cells, rows = sums_ref.shape[2:4]
    odd = me_ref[0] & 1
    towards = jnp.where((me_ref[0] == 0) | (me_ref[0] == tiles - 1), 0, 2 * odd - 1)
    twin_row = pl.multiple_of((1 - odd) * 2 * rows, rows)
    far_row = pl.multiple_of(odd * 2 * rows, rows)
    for epoch in range(epochs):
        for kind in range(2):
            clear_sides(wide_ref, epoch, kind)
            for cell in range(cells):
                index = (epoch * 2 + kind) * cells + cell
                at = wide_ref.at[epoch, kind, cell + 1]
                at[rows : 2 * rows, :] = tile_of(own_refs, index)
                at[pl.ds(twin_row, rows), :] = twin_refs[0][index] + twin_refs[1][index]
                at[pl.ds(far_row, rows), :] = jnp.zeros((rows, LANES), jnp.float32)

    def one_velocity(vel, counts):
        counts = list(counts)
        sums = [[jnp.zeros((rows, LANES), jnp.float32) for _ in range(cells)] for _ in range(2)]
        for epoch in range(epochs):
            row = row_ref[epoch, vel]
            start_col = LANES + col_ref[epoch, vel]
            windows = windows_at(wide_ref, epoch, rows + row, start_col, rows)
            for kind in range(2):
                for cell in range(cells):
                    sums[kind][cell] = sums[kind][cell] + windows[kind][cell]
            part = sum(epoch >= sum(split[: index + 1]) for index in range(PARTS - 1))
            place = epoch - sum(split[:part])
            start_row = row + (1 - odd) * rows
            code = (vel << 24) | (place << 16) | (start_row << 10) | start_col
            list_refs[part][counts[part]] = code
            counts[part] = counts[part] + jnp.where(row * towards > 0, 1, 0)
        for kind in range(2):
            for cell in range(cells):
                sums_ref[vel, kind, cell] = sums[kind][cell]
        return counts

    counts = lax.fori_loop(0, vels, one_velocity, [jnp.int32(0)] * PARTS, unroll=4)
    for part, count in enumerate(counts):
        for index in range(group):
            list_refs[part][count + index] = (((1 - odd) * rows) << 10) | LANES
        count_ref[part] = count
    count_ref[PARTS] = odd


def far_kernel(part, group, list_ref, count_ref, far_ref, given_ref, sums_ref, *refs):
    *best_refs, wide_ref = refs
    vels, _, cells, rows, _ = sums_ref.shape
    odd = count_ref[PARTS]
    far_row = pl.multiple_of(odd * rows, rows)
    zero_row = pl.multiple_of((1 - odd) * rows, rows)
    for epoch in range(wide_ref.shape[0]):
        for kind in range(2):
            clear_sides(wide_ref, epoch, kind)
            for cell in range(cells):
                at = wide_ref.at[epoch, kind, cell + 1]
                at[pl.ds(far_row, rows), :] = far_ref[(epoch * 2 + kind) * cells + cell]
                at[pl.ds(zero_row, rows), :] = jnp.zeros((rows, LANES), jnp.float32)

    def one_group(turn, carry):
        found = []
        for index in range(group):
            code = list_ref[turn * group + index]
            start_col = code & 1023
            start_row = (code >> 10) & 63
            epoch = (code >> 16) & 255
            found.append((code >> 24, windows_at(wide_ref, epoch, start_row, start_col, rows)))
        for vel, windows in found:
            for kind in range(2):
                for cell in range(cells):
                    sums_ref[vel, kind, cell] = sums_ref[vel, kind, cell] + windows[kind][cell]
        return carry

    lax.fori_loop(0, lax.div(count_ref[part] + group - 1, group), one_group, 0)
    for best_ref in best_refs:
        highest = [jnp.full((rows, LANES), -jnp.inf, jnp.float32) for _ in range(cells)]
        for vel in range(vels):
            for cell in range(cells):
                scale = lax.rsqrt(jnp.maximum(sums_ref[vel, 1, cell], 1.0))
                highest[cell] = jnp.maximum(highest[cell], sums_ref[vel, 0, cell] * scale)
        for cell in range(cells):
            best_ref[:, cell * LANES : (cell + 1) * LANES] = highest[cell]


def body(psi, phi, dest_tile, dest_cell, kernel_id, weight, kernels, row_offsets, col_offsets):
    tiles = lax.axis_size("tile")
    cells, epochs, rows, width = psi.shape
    capacity = max(2, 2 * cells * epochs // tiles)
    chips = tiles // 2
    stride = 4 * capacity * rows + 1
    me = lax.axis_index("tile")
    direct = chips <= len(ORDER) + 1
    base = me if direct else me & 1
    given = (jnp.swapaxes(dest_tile, 1, 2), dest_cell, kernel_id, weight, base.reshape(1))
    given += (psi, phi, kernels)
    outputs = chips if direct else 1
    outgoing = pl.pallas_call(
        functools.partial(pack_kernel, capacity, outputs),
        out_shape=[
            jax.ShapeDtypeStruct((chips * stride // outputs, 1, width), jnp.float32)
            for _ in range(outputs)
        ],
        in_specs=[pl.BlockSpec(memory_space=pl.ANY)] * len(given),
        out_specs=[VMEM] * outputs,
        scratch_shapes=[
            pltpu.VMEM((chips * stride, width), jnp.float32),
            pltpu.VMEM((kernels.shape[0], 3, width), jnp.float32),
            pltpu.VMEM((chips, 1, LANES), jnp.float32),
            pltpu.SMEM((tiles,), jnp.int32),
            pltpu.SMEM((cells, epochs), jnp.int32),
        ]
        + [pltpu.SMEM(array.shape, array.dtype) for array in given[:5]]
        + [pltpu.VMEM(array.shape, array.dtype) for array in given[5:]]
        + [pltpu.SemaphoreType.DMA((len(given),))],
        compiler_params=LIMIT,
        name="pack",
    )(*(pltpu.with_memory_space_constraint(array, pltpu.HBM) for array in given))
    if direct:
        incoming = [outgoing[0]] + [
            lax.ppermute(outgoing[k], "tile", [(i, i ^ (2 * k)) for i in range(tiles)])
            for k in ORDER
            if k < chips
        ]
    else:
        incoming = lax.all_to_all(
            outgoing[0].reshape(chips, stride, 1, width),
            "tile",
            split_axis=0,
            concat_axis=0,
            axis_index_groups=[list(range(core, tiles, 2)) for core in range(2)],
            tiled=True,
        )
        incoming = [incoming.reshape(chips * stride, 1, width)]
    total = epochs * 2 * cells
    sky_shape = jax.ShapeDtypeStruct((total, rows, width), jnp.float32)
    skies = []
    for some in (incoming[:EARLY], incoming[EARLY:]):
        if some:
            skies = pl.pallas_call(
                functools.partial(sum_kernel, capacity, cells, not skies),
                out_shape=[sky_shape, sky_shape],
                in_specs=[VMEM] * (len(some) + len(skies)),
                out_specs=[VMEM, VMEM],
                input_output_aliases={len(some) + i: i for i in range(len(skies))},
                compiler_params=LIMIT,
                name="sum_slots",
            )(*some, *skies)
    mine, others = skies
    across = [(i, i ^ 1) for i in range(tiles)]
    other = lax.ppermute(others, "tile", across)
    theirs = lax.ppermute(mine, "tile", across)
    split = [epochs - epochs // 4 - epochs // 8, epochs // 4, epochs // 8]
    own = pl.pallas_call(
        join_kernel,
        out_shape=[
            jax.ShapeDtypeStruct((count * 2 * cells, rows, width), jnp.float32)
            for count in split
        ],
        in_specs=[VMEM, VMEM],
        out_specs=[VMEM] * PARTS,
        compiler_params=LIMIT,
        name="join",
    )(mine, other)
    fields = lax.axis_size("field")
    pairs = [(f * tiles + i, f * tiles + i + 1) for f in range(fields) for i in range(1, tiles - 1, 2)]
    pairs += [
        (f * tiles + i, (f + 1) * tiles + i) for f in range(0, fields - 1, 2) for i in (0, tiles - 1)
    ]
    both = [way for a, b in pairs for way in ((a, b), (b, a))]
    far = [lax.ppermute(part, ("field", "tile"), both) for part in own]
    vels = row_offsets.shape[1]
    sums_shape = jax.ShapeDtypeStruct((vels, 2, cells, rows, width), jnp.float32)
    sums, *lists, count = pl.pallas_call(
        functools.partial(near_kernel, tiles, GROUP, split),
        out_shape=[sums_shape]
        + [pltpu.SMEM((vels * count + GROUP,), jnp.int32) for count in split]
        + [pltpu.SMEM((PARTS + 1,), jnp.int32)],
        in_specs=[SMEM] * 3 + [VMEM] * (PARTS + 2),
        out_specs=[VMEM] + [SMEM] * (PARTS + 1),
        scratch_shapes=[pltpu.VMEM((epochs, 2, cells + 2, 3 * rows, width), jnp.float32)],
        compiler_params=LIMIT,
        name="stack_near",
    )(row_offsets, col_offsets, me.reshape(1), *own, others, theirs)
    for part in range(PARTS):
        last = part == PARTS - 1
        sums, *best = pl.pallas_call(
            functools.partial(far_kernel, part, GROUP),
            out_shape=[sums_shape]
            + [jax.ShapeDtypeStruct((rows, cells * width), jnp.float32)] * last,
            in_specs=[SMEM] * 2 + [VMEM] * 2,
            out_specs=[VMEM] * (1 + last),
            input_output_aliases={3: 0},
            scratch_shapes=[
                pltpu.VMEM((split[part], 2, cells + 2, 2 * rows, width), jnp.float32)
            ],
            compiler_params=LIMIT,
            name="stack_far",
        )(lists[part], count, far[part], sums)
    return best[0]


def solution(mesh):
    placed = (
        P(("field", "tile"), None, None, None),
        P(("field", "tile"), None, None, None),
        P(("field", "tile"), None, None),
        P(("field", "tile"), None),
        P(("field", "tile"), None),
        P(("field", "tile"), None),
        P(),
        P("field", None),
        P("field", None),
    )
    return jax.shard_map(
        body, mesh=mesh, in_specs=placed, out_specs=P(("field", "tile"), None), check_vma=False
    )
```

```python
import functools

import jax
import jax.numpy as jnp
from jax import lax
from jax.experimental import pallas as pl
from jax.experimental.pallas import tpu as pltpu
from jax.sharding import PartitionSpec as P

XREACH = 64
RREACH = 8
LANES = 128
GROUP = 16
PARTS = 3
EARLY = 6
ORDER = (4, 2, 5, 3, 7, 6, 1)
VMEM = pl.BlockSpec(memory_space=pltpu.VMEM)
SMEM = pl.BlockSpec(memory_space=pltpu.SMEM)
LIMIT = pltpu.CompilerParams(vmem_limit_bytes=32 * 1024 * 1024)


def pack_kernel(capacity, outputs, *refs):
    given, out_refs, rest = refs[:8], refs[8 : 8 + outputs], refs[8 + outputs :]
    (slots_ref, diag_ref, note_ref, used_ref, spot_ref), held, sems = rest[:5], rest[5:13], rest[13]
    copies = [
        pltpu.make_async_copy(source, target, sems.at[index])
        for index, (source, target) in enumerate(zip(given, held, strict=True))
    ]
    for copy in copies[::-1]:
        copy.start()
    tile_ref, cell_ref, id_ref, weight_ref, base_ref, psi_ref, phi_ref, table_ref = held
    cells, epochs, rows, width = psi_ref.shape
    chips = note_ref.shape[0]
    stride = 4 * capacity * rows + 1

    def clear(tile, carry):
        used_ref[tile] = 0
        return carry

    lax.fori_loop(0, used_ref.shape[0], clear, 0, unroll=16)
    note_ref[...] = jnp.zeros(note_ref.shape, jnp.float32)
    for copy in copies[:5]:
        copy.wait()

    lane = lax.broadcasted_iota(jnp.int32, (1, LANES), 1)
    for block in range(cells):
        for epoch in range(epochs):
            tile = tile_ref[block, 0, epoch] ^ base_ref[0]
            chip, core = tile >> 1, tile & 1
            slot = used_ref[tile]
            used_ref[tile] = slot + 1
            slot = core * capacity + slot
            spot_ref[block, epoch] = chip * stride + 2 * rows * slot
            place = (epoch * 2 * cells + cell_ref[block, epoch] + 1).astype(jnp.float32)
            note_ref[chip] = jnp.where(lane == slot, place, note_ref[chip])
    for copy in copies[5:]:
        copy.wait()

    source = lax.broadcasted_iota(jnp.int32, (width, width), 0)
    target = lax.broadcasted_iota(jnp.int32, (width, width), 1)
    for place in range(3):
        mask = source == target + (place - 1)
        for index in range(table_ref.shape[0]):
            row = jnp.sum(jnp.where(mask, table_ref[index], 0.0), axis=0, keepdims=True)
            diag_ref[index, place : place + 1, :] = row

    def write_note(chip, carry):
        slots_ref[pl.ds(chip * stride + stride - 1, 1), :] = note_ref[chip]
        return carry

    lax.fori_loop(0, chips, write_note, 0, unroll=8)
    for block in range(cells):
        for epoch in range(epochs):
            spot = spot_ref[block, epoch]
            bands = diag_ref[id_ref[block, epoch]] * weight_ref[block, epoch]
            for kind, ref in enumerate((psi_ref, phi_ref)):
                values = ref[block, epoch]
                slots_ref[pl.ds(spot + kind * rows, rows), :] = (
                    values * bands[1:2]
                    + pltpu.roll(values, 1, 1) * bands[0:1]
                    + pltpu.roll(values, width - 1, 1) * bands[2:3]
                )
    first = 0
    for out_ref in out_refs:
        count = out_ref.shape[0]
        flat_ref = out_ref.reshape(count, width)
        for row in range(0, count, rows):
            size = min(rows, count - row)
            flat_ref[row : row + size, :] = slots_ref[first + row : first + row + size, :]
        first += count


def sum_kernel(capacity, cells, first_call, sides, *refs):
    skies = len(sides)
    in_refs, sky_refs = refs[: -skies if first_call else -2 * skies], refs[-skies:]
    rows, width = sky_refs[0].shape[1:]
    stride = 4 * capacity * rows + 1
    for sky_ref in sky_refs if first_call else ():
        for index in range(sky_ref.shape[0]):
            sky_ref[index] = jnp.zeros((rows, width), jnp.float32)
    for in_ref in in_refs:
        flat_ref = in_ref.reshape(in_ref.shape[0], width)

        def one_message(message, carry, flat_ref=flat_ref):
            first = message * stride
            notes = flat_ref[pl.ds(first + stride - 1, 1), :].astype(jnp.int32)
            for slot in (side * capacity + rank for side in sides for rank in range(capacity)):
                sky_ref = sky_refs[sides.index(slot // capacity)]
                place = notes[0, slot] - 1
                there = place >= 0
                base = jnp.maximum(place, 0)
                for kind in range(2):
                    value = flat_ref[pl.ds(first + (2 * slot + kind) * rows, rows), :]
                    value = jnp.where(there, value, 0.0)
                    sky_ref[base + kind * cells] = sky_ref[base + kind * cells] + value
            return carry

        messages = in_ref.shape[0] // stride
        if messages == 1:
            one_message(0, 0)
        else:
            lax.fori_loop(0, messages, one_message, 0, unroll=8)


def join_kernel(mine_ref, other_ref, *part_refs):
    first = 0
    for part_ref in part_refs:
        for index in range(part_ref.shape[0]):
            part_ref[index] = mine_ref[first + index] + other_ref[first + index]
        first += part_ref.shape[0]


def windows_at(ref, epoch, start_row, start_col, rows):
    first = lax.shift_right_logical(start_col, 7)
    shift = start_col & (LANES - 1)
    turn = (LANES - shift) & (LANES - 1)
    mask = lax.broadcasted_iota(jnp.int32, (rows, LANES), 1) >= shift
    windows = []
    for kind in range(2):
        parts = [
            ref[epoch, kind, first + step, pl.ds(start_row, rows), :]
            for step in range(ref.shape[2] - 1)
        ]
        windows.append(
            [
                pltpu.roll(jnp.where(mask, parts[cell], parts[cell + 1]), turn, 1)
                for cell in range(len(parts) - 1)
            ]
        )
    return windows


def clear_sides(ref, epoch, kind):
    for side in (0, ref.shape[2] - 1):
        ref[epoch, kind, side] = jnp.zeros(ref.shape[3:], jnp.float32)


def tile_of(refs, index):
    for ref in refs:
        if index < ref.shape[0]:
            return ref[index]
        index -= ref.shape[0]


def near_kernel(tiles, group, split, row_ref, col_ref, me_ref, *refs):
    own_refs, twin_refs = refs[:PARTS], refs[PARTS : PARTS + 2]
    sums_ref, *list_refs, count_ref, wide_ref = refs[PARTS + 2 :]
    epochs, vels = row_ref.shape
    cells, rows = sums_ref.shape[2:4]
    odd = me_ref[0] & 1
    towards = jnp.where((me_ref[0] == 0) | (me_ref[0] == tiles - 1), 0, 2 * odd - 1)
    twin_row = pl.multiple_of((1 - odd) * 2 * rows, rows)
    far_row = pl.multiple_of(odd * 2 * rows, rows)
    for epoch in range(epochs):
        for kind in range(2):
            clear_sides(wide_ref, epoch, kind)
            for cell in range(cells):
                index = (epoch * 2 + kind) * cells + cell
                at = wide_ref.at[epoch, kind, cell + 1]
                at[rows : 2 * rows, :] = tile_of(own_refs, index)
                at[pl.ds(twin_row, rows), :] = twin_refs[0][index] + twin_refs[1][index]
                at[pl.ds(far_row, rows), :] = jnp.zeros((rows, LANES), jnp.float32)

    def one_velocity(vel, counts):
        counts = list(counts)
        sums = [[jnp.zeros((rows, LANES), jnp.float32) for _ in range(cells)] for _ in range(2)]
        for epoch in range(epochs):
            row = row_ref[epoch, vel]
            start_col = LANES + col_ref[epoch, vel]
            windows = windows_at(wide_ref, epoch, rows + row, start_col, rows)
            for kind in range(2):
                for cell in range(cells):
                    sums[kind][cell] = sums[kind][cell] + windows[kind][cell]
            part = sum(epoch >= sum(split[: index + 1]) for index in range(PARTS - 1))
            place = epoch - sum(split[:part])
            start_row = row + (1 - odd) * rows
            code = (vel << 24) | (place << 16) | (start_row << 10) | start_col
            list_refs[part][counts[part]] = code
            counts[part] = counts[part] + jnp.where(row * towards > 0, 1, 0)
        for kind in range(2):
            for cell in range(cells):
                sums_ref[vel, kind, cell] = sums[kind][cell]
        return counts

    counts = lax.fori_loop(0, vels, one_velocity, [jnp.int32(0)] * PARTS, unroll=4)
    for part, count in enumerate(counts):
        for index in range(group):
            list_refs[part][count + index] = (((1 - odd) * rows) << 10) | LANES
        count_ref[part] = count
    count_ref[PARTS] = odd


def far_kernel(part, group, list_ref, count_ref, far_ref, given_ref, sums_ref, *refs):
    *best_refs, wide_ref = refs
    vels, _, cells, rows, _ = sums_ref.shape
    odd = count_ref[PARTS]
    far_row = pl.multiple_of(odd * rows, rows)
    zero_row = pl.multiple_of((1 - odd) * rows, rows)
    for epoch in range(wide_ref.shape[0]):
        for kind in range(2):
            clear_sides(wide_ref, epoch, kind)
            for cell in range(cells):
                at = wide_ref.at[epoch, kind, cell + 1]
                at[pl.ds(far_row, rows), :] = far_ref[(epoch * 2 + kind) * cells + cell]
                at[pl.ds(zero_row, rows), :] = jnp.zeros((rows, LANES), jnp.float32)

    def one_group(turn, carry):
        found = []
        for index in range(group):
            code = list_ref[turn * group + index]
            start_col = code & 1023
            start_row = (code >> 10) & 63
            epoch = (code >> 16) & 255
            found.append((code >> 24, windows_at(wide_ref, epoch, start_row, start_col, rows)))
        for vel, windows in found:
            for kind in range(2):
                for cell in range(cells):
                    sums_ref[vel, kind, cell] = sums_ref[vel, kind, cell] + windows[kind][cell]
        return carry

    lax.fori_loop(0, lax.div(count_ref[part] + group - 1, group), one_group, 0)
    for best_ref in best_refs:
        highest = [jnp.full((rows, LANES), -jnp.inf, jnp.float32) for _ in range(cells)]
        for vel in range(vels):
            for cell in range(cells):
                scale = lax.rsqrt(jnp.maximum(sums_ref[vel, 1, cell], 1.0))
                highest[cell] = jnp.maximum(highest[cell], sums_ref[vel, 0, cell] * scale)
        for cell in range(cells):
            best_ref[:, cell * LANES : (cell + 1) * LANES] = highest[cell]


def body(psi, phi, dest_tile, dest_cell, kernel_id, weight, kernels, row_offsets, col_offsets):
    tiles = lax.axis_size("tile")
    cells, epochs, rows, width = psi.shape
    capacity = max(2, 2 * cells * epochs // tiles)
    chips = tiles // 2
    stride = 4 * capacity * rows + 1
    me = lax.axis_index("tile")
    direct = chips <= len(ORDER) + 1
    base = me if direct else me & 1
    given = (jnp.swapaxes(dest_tile, 1, 2), dest_cell, kernel_id, weight, base.reshape(1))
    given += (psi, phi, kernels)
    outputs = chips if direct else 1
    outgoing = pl.pallas_call(
        functools.partial(pack_kernel, capacity, outputs),
        out_shape=[
            jax.ShapeDtypeStruct((chips * stride // outputs, 1, width), jnp.float32)
            for _ in range(outputs)
        ],
        in_specs=[pl.BlockSpec(memory_space=pl.ANY)] * len(given),
        out_specs=[VMEM] * outputs,
        scratch_shapes=[
            pltpu.VMEM((chips * stride, width), jnp.float32),
            pltpu.VMEM((kernels.shape[0], 3, width), jnp.float32),
            pltpu.VMEM((chips, 1, LANES), jnp.float32),
            pltpu.SMEM((tiles,), jnp.int32),
            pltpu.SMEM((cells, epochs), jnp.int32),
        ]
        + [pltpu.SMEM(array.shape, array.dtype) for array in given[:5]]
        + [pltpu.VMEM(array.shape, array.dtype) for array in given[5:]]
        + [pltpu.SemaphoreType.DMA((len(given),))],
        compiler_params=LIMIT,
        name="pack",
    )(*(pltpu.with_memory_space_constraint(array, pltpu.HBM) for array in given))
    if direct:
        incoming = [outgoing[0]] + [
            lax.ppermute(outgoing[k], "tile", [(i, i ^ (2 * k)) for i in range(tiles)])
            for k in ORDER
            if k < chips
        ]
    else:
        incoming = lax.all_to_all(
            outgoing[0].reshape(chips, stride, 1, width),
            "tile",
            split_axis=0,
            concat_axis=0,
            axis_index_groups=[list(range(core, tiles, 2)) for core in range(2)],
            tiled=True,
        )
        incoming = [incoming.reshape(chips * stride, 1, width)]
    total = epochs * 2 * cells
    sky_shape = jax.ShapeDtypeStruct((total, rows, width), jnp.float32)
    def summed(some, sides, skies=()):
        return pl.pallas_call(
            functools.partial(sum_kernel, capacity, cells, not skies, sides),
            out_shape=[sky_shape] * len(sides),
            in_specs=[VMEM] * (len(some) + len(skies)),
            out_specs=[VMEM] * len(sides),
            input_output_aliases={len(some) + i: i for i in range(len(skies))},
            compiler_params=LIMIT,
            name="sum_slots",
        )(*some, *skies)

    mine, others = summed(incoming[:EARLY], (0, 1))
    if incoming[EARLY:]:
        (others,) = summed(incoming[EARLY:], (1,), (others,))
        (mine,) = summed(incoming[EARLY:], (0,), (mine,))
    across = [(i, i ^ 1) for i in range(tiles)]
    other = lax.ppermute(others, "tile", across)
    theirs = lax.ppermute(mine, "tile", across)
    split = [epochs - epochs // 4 - epochs // 8, epochs // 4, epochs // 8]
    own = pl.pallas_call(
        join_kernel,
        out_shape=[
            jax.ShapeDtypeStruct((count * 2 * cells, rows, width), jnp.float32)
            for count in split
        ],
        in_specs=[VMEM, VMEM],
        out_specs=[VMEM] * PARTS,
        compiler_params=LIMIT,
        name="join",
    )(mine, other)
    fields = lax.axis_size("field")
    pairs = [(f * tiles + i, f * tiles + i + 1) for f in range(fields) for i in range(1, tiles - 1, 2)]
    pairs += [
        (f * tiles + i, (f + 1) * tiles + i) for f in range(0, fields - 1, 2) for i in (0, tiles - 1)
    ]
    both = [way for a, b in pairs for way in ((a, b), (b, a))]
    far = [lax.ppermute(part, ("field", "tile"), both) for part in own]
    vels = row_offsets.shape[1]
    sums_shape = jax.ShapeDtypeStruct((vels, 2, cells, rows, width), jnp.float32)
    sums, *lists, count = pl.pallas_call(
        functools.partial(near_kernel, tiles, GROUP, split),
        out_shape=[sums_shape]
        + [pltpu.SMEM((vels * count + GROUP,), jnp.int32) for count in split]
        + [pltpu.SMEM((PARTS + 1,), jnp.int32)],
        in_specs=[SMEM] * 3 + [VMEM] * (PARTS + 2),
        out_specs=[VMEM] + [SMEM] * (PARTS + 1),
        scratch_shapes=[pltpu.VMEM((epochs, 2, cells + 2, 3 * rows, width), jnp.float32)],
        compiler_params=LIMIT,
        name="stack_near",
    )(row_offsets, col_offsets, me.reshape(1), *own, others, theirs)
    for part in range(PARTS):
        last = part == PARTS - 1
        sums, *best = pl.pallas_call(
            functools.partial(far_kernel, part, GROUP),
            out_shape=[sums_shape]
            + [jax.ShapeDtypeStruct((rows, cells * width), jnp.float32)] * last,
            in_specs=[SMEM] * 2 + [VMEM] * 2,
            out_specs=[VMEM] * (1 + last),
            input_output_aliases={3: 0},
            scratch_shapes=[
                pltpu.VMEM((split[part], 2, cells + 2, 2 * rows, width), jnp.float32)
            ],
            compiler_params=LIMIT,
            name="stack_far",
        )(lists[part], count, far[part], sums)
    return best[0]


def solution(mesh):
    placed = (
        P(("field", "tile"), None, None, None),
        P(("field", "tile"), None, None, None),
        P(("field", "tile"), None, None),
        P(("field", "tile"), None),
        P(("field", "tile"), None),
        P(("field", "tile"), None),
        P(),
        P("field", None),
        P("field", None),
    )
    return jax.shard_map(
        body, mesh=mesh, in_specs=placed, out_specs=P(("field", "tile"), None), check_vma=False
    )
```

```python
import functools

import jax
import jax.numpy as jnp
from jax import lax
from jax.experimental import pallas as pl
from jax.experimental.pallas import tpu as pltpu
from jax.sharding import PartitionSpec as P

XREACH = 64
RREACH = 8
LANES = 128
GROUP = 12
PARTS = 3
EARLY = 6
ORDER = (4, 2, 5, 3, 7, 6, 1)
VMEM = pl.BlockSpec(memory_space=pltpu.VMEM)
SMEM = pl.BlockSpec(memory_space=pltpu.SMEM)
LIMIT = pltpu.CompilerParams(vmem_limit_bytes=32 * 1024 * 1024)


def pack_kernel(capacity, outputs, *refs):
    given, out_refs, rest = refs[:8], refs[8 : 8 + outputs], refs[8 + outputs :]
    (slots_ref, diag_ref, note_ref, used_ref, spot_ref), held, sems = rest[:5], rest[5:13], rest[13]
    copies = [
        pltpu.make_async_copy(source, target, sems.at[index])
        for index, (source, target) in enumerate(zip(given, held, strict=True))
    ]
    for copy in copies[::-1]:
        copy.start()
    tile_ref, cell_ref, id_ref, weight_ref, base_ref, psi_ref, phi_ref, table_ref = held
    cells, epochs, rows, width = psi_ref.shape
    chips = note_ref.shape[0]
    stride = 4 * capacity * rows + 1

    def clear(tile, carry):
        used_ref[tile] = 0
        return carry

    lax.fori_loop(0, used_ref.shape[0], clear, 0, unroll=16)
    note_ref[...] = jnp.zeros(note_ref.shape, jnp.float32)
    for copy in copies[:5]:
        copy.wait()

    lane = lax.broadcasted_iota(jnp.int32, (1, LANES), 1)
    for block in range(cells):
        for epoch in range(epochs):
            tile = tile_ref[block, 0, epoch] ^ base_ref[0]
            chip, core = tile >> 1, tile & 1
            slot = used_ref[tile]
            used_ref[tile] = slot + 1
            slot = core * capacity + slot
            spot_ref[block, epoch] = chip * stride + 2 * rows * slot
            place = (epoch * 2 * cells + cell_ref[block, epoch] + 1).astype(jnp.float32)
            note_ref[chip] = jnp.where(lane == slot, place, note_ref[chip])
    for copy in copies[5:]:
        copy.wait()

    source = lax.broadcasted_iota(jnp.int32, (width, width), 0)
    target = lax.broadcasted_iota(jnp.int32, (width, width), 1)
    for place in range(3):
        mask = source == target + (place - 1)
        for index in range(table_ref.shape[0]):
            row = jnp.sum(jnp.where(mask, table_ref[index], 0.0), axis=0, keepdims=True)
            diag_ref[index, place : place + 1, :] = row

    def write_note(chip, carry):
        slots_ref[pl.ds(chip * stride + stride - 1, 1), :] = note_ref[chip]
        return carry

    lax.fori_loop(0, chips, write_note, 0, unroll=8)
    for block in range(cells):
        for epoch in range(epochs):
            spot = spot_ref[block, epoch]
            bands = diag_ref[id_ref[block, epoch]] * weight_ref[block, epoch]
            for kind, ref in enumerate((psi_ref, phi_ref)):
                values = ref[block, epoch]
                slots_ref[pl.ds(spot + kind * rows, rows), :] = (
                    values * bands[1:2]
                    + pltpu.roll(values, 1, 1) * bands[0:1]
                    + pltpu.roll(values, width - 1, 1) * bands[2:3]
                )
    first = 0
    for out_ref in out_refs:
        count = out_ref.shape[0]
        flat_ref = out_ref.reshape(count, width)
        for row in range(0, count, rows):
            size = min(rows, count - row)
            flat_ref[row : row + size, :] = slots_ref[first + row : first + row + size, :]
        first += count


def sum_kernel(capacity, cells, first_call, *refs):
    in_refs, sky_refs = refs[: -2 if first_call else -4], refs[-2:]
    rows, width = sky_refs[0].shape[1:]
    stride = 4 * capacity * rows + 1
    for sky_ref in sky_refs if first_call else ():
        for index in range(sky_ref.shape[0]):
            sky_ref[index] = jnp.zeros((rows, width), jnp.float32)
    for in_ref in in_refs:
        flat_ref = in_ref.reshape(in_ref.shape[0], width)

        def one_message(message, carry, flat_ref=flat_ref):
            first = message * stride
            notes = flat_ref[pl.ds(first + stride - 1, 1), :].astype(jnp.int32)
            for slot in range(2 * capacity):
                sky_ref = sky_refs[slot // capacity]
                place = notes[0, slot] - 1
                there = place >= 0
                base = jnp.maximum(place, 0)
                for kind in range(2):
                    value = flat_ref[pl.ds(first + (2 * slot + kind) * rows, rows), :]
                    value = jnp.where(there, value, 0.0)
                    sky_ref[base + kind * cells] = sky_ref[base + kind * cells] + value
            return carry

        messages = in_ref.shape[0] // stride
        if messages == 1:
            one_message(0, 0)
        else:
            lax.fori_loop(0, messages, one_message, 0, unroll=8)


def join_kernel(mine_ref, other_ref, *part_refs):
    first = 0
    for part_ref in part_refs:
        for index in range(part_ref.shape[0]):
            part_ref[index] = mine_ref[first + index] + other_ref[first + index]
        first += part_ref.shape[0]


def windows_at(ref, epoch, start_row, start_col, rows):
    first = lax.shift_right_logical(start_col, 7)
    shift = start_col & (LANES - 1)
    turn = (LANES - shift) & (LANES - 1)
    mask = lax.broadcasted_iota(jnp.int32, (rows, LANES), 1) >= shift
    windows = []
    for kind in range(2):
        parts = [
            ref[epoch, kind, first + step, pl.ds(start_row, rows), :]
            for step in range(ref.shape[2] - 1)
        ]
        windows.append(
            [
                pltpu.roll(jnp.where(mask, parts[cell], parts[cell + 1]), turn, 1)
                for cell in range(len(parts) - 1)
            ]
        )
    return windows


def clear_sides(ref, epoch, kind):
    for side in (0, ref.shape[2] - 1):
        ref[epoch, kind, side] = jnp.zeros(ref.shape[3:], jnp.float32)


def tile_of(refs, index):
    for ref in refs:
        if index < ref.shape[0]:
            return ref[index]
        index -= ref.shape[0]


def near_kernel(tiles, group, split, row_ref, col_ref, me_ref, *refs):
    own_refs, twin_refs = refs[:PARTS], refs[PARTS : PARTS + 2]
    sums_ref, *list_refs, count_ref, wide_ref = refs[PARTS + 2 :]
    epochs, vels = row_ref.shape
    cells, rows = sums_ref.shape[2:4]
    odd = me_ref[0] & 1
    towards = jnp.where((me_ref[0] == 0) | (me_ref[0] == tiles - 1), 0, 2 * odd - 1)
    twin_row = pl.multiple_of((1 - odd) * 2 * rows, rows)
    far_row = pl.multiple_of(odd * 2 * rows, rows)
    for epoch in range(epochs):
        for kind in range(2):
            clear_sides(wide_ref, epoch, kind)
            for cell in range(cells):
                index = (epoch * 2 + kind) * cells + cell
                at = wide_ref.at[epoch, kind, cell + 1]
                at[rows : 2 * rows, :] = tile_of(own_refs, index)
                at[pl.ds(twin_row, rows), :] = twin_refs[0][index] + twin_refs[1][index]
                at[pl.ds(far_row, rows), :] = jnp.zeros((rows, LANES), jnp.float32)

    def one_velocity(vel, counts):
        counts = list(counts)
        sums = [[jnp.zeros((rows, LANES), jnp.float32) for _ in range(cells)] for _ in range(2)]
        for epoch in range(epochs):
            row = row_ref[epoch, vel]
            start_col = LANES + col_ref[epoch, vel]
            windows = windows_at(wide_ref, epoch, rows + row, start_col, rows)
            for kind in range(2):
                for cell in range(cells):
                    sums[kind][cell] = sums[kind][cell] + windows[kind][cell]
            part = sum(epoch >= sum(split[: index + 1]) for index in range(PARTS - 1))
            place = epoch - sum(split[:part])
            start_row = row + (1 - odd) * rows
            code = (vel << 24) | (place << 16) | (start_row << 10) | start_col
            list_refs[part][counts[part]] = code
            counts[part] = counts[part] + jnp.where(row * towards > 0, 1, 0)
        for kind in range(2):
            for cell in range(cells):
                sums_ref[vel, kind, cell] = sums[kind][cell]
        return counts

    counts = lax.fori_loop(0, vels, one_velocity, [jnp.int32(0)] * PARTS, unroll=4)
    for part, count in enumerate(counts):
        for index in range(group):
            list_refs[part][count + index] = (((1 - odd) * rows) << 10) | LANES
        count_ref[part] = count
    count_ref[PARTS] = odd


def far_kernel(part, group, list_ref, count_ref, far_ref, given_ref, sums_ref, *refs):
    *best_refs, wide_ref = refs
    vels, _, cells, rows, _ = sums_ref.shape
    odd = count_ref[PARTS]
    far_row = pl.multiple_of(odd * rows, rows)
    zero_row = pl.multiple_of((1 - odd) * rows, rows)
    for epoch in range(wide_ref.shape[0]):
        for kind in range(2):
            clear_sides(wide_ref, epoch, kind)
            for cell in range(cells):
                at = wide_ref.at[epoch, kind, cell + 1]
                at[pl.ds(far_row, rows), :] = far_ref[(epoch * 2 + kind) * cells + cell]
                at[pl.ds(zero_row, rows), :] = jnp.zeros((rows, LANES), jnp.float32)

    def one_group(turn, carry):
        found = []
        for index in range(group):
            code = list_ref[turn * group + index]
            start_col = code & 1023
            start_row = (code >> 10) & 63
            epoch = (code >> 16) & 255
            found.append((code >> 24, windows_at(wide_ref, epoch, start_row, start_col, rows)))
        for vel, windows in found:
            for kind in range(2):
                for cell in range(cells):
                    sums_ref[vel, kind, cell] = sums_ref[vel, kind, cell] + windows[kind][cell]
        return carry

    lax.fori_loop(0, lax.div(count_ref[part] + group - 1, group), one_group, 0)
    for best_ref in best_refs:
        highest = [jnp.full((rows, LANES), -jnp.inf, jnp.float32) for _ in range(cells)]
        for vel in range(vels):
            for cell in range(cells):
                scale = lax.rsqrt(jnp.maximum(sums_ref[vel, 1, cell], 1.0))
                highest[cell] = jnp.maximum(highest[cell], sums_ref[vel, 0, cell] * scale)
        for cell in range(cells):
            best_ref[:, cell * LANES : (cell + 1) * LANES] = highest[cell]


def body(psi, phi, dest_tile, dest_cell, kernel_id, weight, kernels, row_offsets, col_offsets):
    tiles = lax.axis_size("tile")
    cells, epochs, rows, width = psi.shape
    capacity = max(2, 2 * cells * epochs // tiles)
    chips = tiles // 2
    stride = 4 * capacity * rows + 1
    me = lax.axis_index("tile")
    direct = chips <= len(ORDER) + 1
    base = me if direct else me & 1
    given = (jnp.swapaxes(dest_tile, 1, 2), dest_cell, kernel_id, weight, base.reshape(1))
    given += (psi, phi, kernels)
    outputs = chips if direct else 1
    outgoing = pl.pallas_call(
        functools.partial(pack_kernel, capacity, outputs),
        out_shape=[
            jax.ShapeDtypeStruct((chips * stride // outputs, 1, width), jnp.float32)
            for _ in range(outputs)
        ],
        in_specs=[pl.BlockSpec(memory_space=pl.ANY)] * len(given),
        out_specs=[VMEM] * outputs,
        scratch_shapes=[
            pltpu.VMEM((chips * stride, width), jnp.float32),
            pltpu.VMEM((kernels.shape[0], 3, width), jnp.float32),
            pltpu.VMEM((chips, 1, LANES), jnp.float32),
            pltpu.SMEM((tiles,), jnp.int32),
            pltpu.SMEM((cells, epochs), jnp.int32),
        ]
        + [pltpu.SMEM(array.shape, array.dtype) for array in given[:5]]
        + [pltpu.VMEM(array.shape, array.dtype) for array in given[5:]]
        + [pltpu.SemaphoreType.DMA((len(given),))],
        compiler_params=LIMIT,
        name="pack",
    )(*(pltpu.with_memory_space_constraint(array, pltpu.HBM) for array in given))
    if direct:
        incoming = [outgoing[0]] + [
            lax.ppermute(outgoing[k], "tile", [(i, i ^ (2 * k)) for i in range(tiles)])
            for k in ORDER
            if k < chips
        ]
    else:
        incoming = lax.all_to_all(
            outgoing[0].reshape(chips, stride, 1, width),
            "tile",
            split_axis=0,
            concat_axis=0,
            axis_index_groups=[list(range(core, tiles, 2)) for core in range(2)],
            tiled=True,
        )
        incoming = [incoming.reshape(chips * stride, 1, width)]
    total = epochs * 2 * cells
    sky_shape = jax.ShapeDtypeStruct((total, rows, width), jnp.float32)
    skies = []
    for some in (incoming[:EARLY], incoming[EARLY:]):
        if some:
            skies = pl.pallas_call(
                functools.partial(sum_kernel, capacity, cells, not skies),
                out_shape=[sky_shape, sky_shape],
                in_specs=[VMEM] * (len(some) + len(skies)),
                out_specs=[VMEM, VMEM],
                input_output_aliases={len(some) + i: i for i in range(len(skies))},
                compiler_params=LIMIT,
                name="sum_slots",
            )(*some, *skies)
    mine, others = skies
    across = [(i, i ^ 1) for i in range(tiles)]
    other = lax.ppermute(others, "tile", across)
    theirs = lax.ppermute(mine, "tile", across)
    split = [epochs - epochs // 4 - epochs // 8, epochs // 4, epochs // 8]
    own = pl.pallas_call(
        join_kernel,
        out_shape=[
            jax.ShapeDtypeStruct((count * 2 * cells, rows, width), jnp.float32)
            for count in split
        ],
        in_specs=[VMEM, VMEM],
        out_specs=[VMEM] * PARTS,
        compiler_params=LIMIT,
        name="join",
    )(mine, other)
    fields = lax.axis_size("field")
    pairs = [(f * tiles + i, f * tiles + i + 1) for f in range(fields) for i in range(1, tiles - 1, 2)]
    pairs += [
        (f * tiles + i, (f + 1) * tiles + i) for f in range(0, fields - 1, 2) for i in (0, tiles - 1)
    ]
    both = [way for a, b in pairs for way in ((a, b), (b, a))]
    far = [lax.ppermute(part, ("field", "tile"), both) for part in own]
    vels = row_offsets.shape[1]
    sums_shape = jax.ShapeDtypeStruct((vels, 2, cells, rows, width), jnp.float32)
    sums, *lists, count = pl.pallas_call(
        functools.partial(near_kernel, tiles, GROUP, split),
        out_shape=[sums_shape]
        + [pltpu.SMEM((vels * count + GROUP,), jnp.int32) for count in split]
        + [pltpu.SMEM((PARTS + 1,), jnp.int32)],
        in_specs=[SMEM] * 3 + [VMEM] * (PARTS + 2),
        out_specs=[VMEM] + [SMEM] * (PARTS + 1),
        scratch_shapes=[pltpu.VMEM((epochs, 2, cells + 2, 3 * rows, width), jnp.float32)],
        compiler_params=LIMIT,
        name="stack_near",
    )(row_offsets, col_offsets, me.reshape(1), *own, others, theirs)
    for part in range(PARTS):
        last = part == PARTS - 1
        sums, *best = pl.pallas_call(
            functools.partial(far_kernel, part, GROUP),
            out_shape=[sums_shape]
            + [jax.ShapeDtypeStruct((rows, cells * width), jnp.float32)] * last,
            in_specs=[SMEM] * 2 + [VMEM] * 2,
            out_specs=[VMEM] * (1 + last),
            input_output_aliases={3: 0},
            scratch_shapes=[
                pltpu.VMEM((split[part], 2, cells + 2, 2 * rows, width), jnp.float32)
            ],
            compiler_params=LIMIT,
            name="stack_far",
        )(lists[part], count, far[part], sums)
    return best[0]


def solution(mesh):
    placed = (
        P(("field", "tile"), None, None, None),
        P(("field", "tile"), None, None, None),
        P(("field", "tile"), None, None),
        P(("field", "tile"), None),
        P(("field", "tile"), None),
        P(("field", "tile"), None),
        P(),
        P("field", None),
        P("field", None),
    )
    return jax.shard_map(
        body, mesh=mesh, in_specs=placed, out_specs=P(("field", "tile"), None), check_vma=False
    )
```
